256 devices in a mesh: branch: 2 (over z_lo), seq: 128 (over y, x, z_hi, core).
Axes of the slice: x: 4, y: 4, z: 8 (z_hi: 4, z_lo: 2; z = z_hi * 2 + z_lo), core: 2. Of those that a mesh axis runs over, the one named last changes fastest.
Arguments:
- queries: bfloat16 [4, 2048, 5120], P('branch', 'seq'), may hold values from -40 to 40
- keys: bfloat16 [4, 2048, 5120], P('branch', 'seq'), may hold values from -8 to 8
- values: bfloat16 [4, 2048, 5120], P('branch', 'seq'), may hold values from -6 to 6
- output_weight_matrix: bfloat16 [5120, 5120], P('seq'), may hold values from -0.078125 to 0.078125
- style_down_maps: bfloat16 [4, 5120, 64], P(None, 'seq'), may hold values from -0.078125 to 0.078125
- style_up_maps: bfloat16 [4, 64, 5120], replicated, may hold values from -0.75 to 0.75
- branch_adapter: int32 [4], replicated, may hold values from 0 to 3
- guidance_weight_eighths: int32 [4], replicated, may hold values from -8 to 24
- gate_offset_learned: float32 [5120], P('branch'), may hold values from -3 to 3
- timestep: int32 [1], replicated, may hold values from 0 to 999
Outputs:
- guided: bfloat16 [2048, 5120], P('seq', 'branch')
The draws below stay inside these ranges and needn't reach their ends.
All inputs are finite; a program needn't handle non-finite values.
Results may differ from the reference program's by a relative error of at most 0.019.
Values may be sent and summed in bfloat16 or wider, within the bound.
A program may use at most 128 MiB of HBM per device.

```python
import math
import jax
import jax.numpy as jnp
from jax import lax

MODEL_WIDTH = 5120
HEADS = 40
HEAD_DIM = 128
UDEG = 8
BRANCHES = 4
STYLE_ADAPTERS = 4
ADAPTER_RANK = 64
TOKENS = 2048


def drawn_places(key):
    first_key = jax.random.fold_in(key, 5)
    starts = jax.random.randint(first_key, (2, BRANCHES, 1), 0, TOKENS)
    spacing = jnp.arange(3, dtype=jnp.int32)[None, :] * (TOKENS // 8)
    key_places = (starts[0] + spacing) % TOKENS
    return key_places


def shared_keys(key):
    first_key = jax.random.fold_in(key, 11)
    gaussian = jnp.clip(jax.random.normal(first_key, (BRANCHES, TOKENS, MODEL_WIDTH), jnp.float32), -4.0, 4.0)
    key_field = 2.0 * gaussian
    key_places = drawn_places(key)
    twin_places = (key_places + TOKENS // 2) % TOKENS
    branch_rows = jnp.arange(BRANCHES, dtype=jnp.int32)[:, None]
    twin_value = key_field[branch_rows, twin_places]
    key_field = key_field.at[branch_rows, twin_places].set(twin_value)
    return key_field


def draw_keys(key, part):
    key_field = shared_keys(key)
    return key_field.astype(jnp.bfloat16)


def draw_queries(key, part):
    own_key = jax.random.fold_in(key, 3)
    query_field = 2.0 * jnp.clip(jax.random.normal(own_key, (BRANCHES, TOKENS, MODEL_WIDTH), jnp.float32), -4.0, 4.0)
    return query_field.astype(jnp.bfloat16)


def place_ends(values, stream_key, least, largest):
    extent = values.shape
    index_at = [jax.random.randint(jax.random.fold_in(stream_key, axis), (), 0, extent[axis]) for axis in range(len(extent))]
    values = values.at[tuple(index_at)].set(least)
    longest = extent.index(max(extent))
    index_at[longest] = (index_at[longest] + 1) % extent[longest]
    return values.at[tuple(index_at)].set(largest)


def block_scale(stream_key, shape, pieces, smallest, largest):
    def one(position, blocks):
        draws = jax.random.uniform(jax.random.fold_in(jax.random.fold_in(stream_key, 6), position), (blocks,), jnp.float32, smallest / len(pieces), largest / len(pieces))
        return jnp.repeat(jnp.exp(draws), shape[position] // blocks).reshape((-1,) + (1,) * (len(shape) - position - 1))

    level = one(*pieces[0])
    for cut in pieces[1:]:
        level = level * one(*cut)
    return level


def noise(key, extent, width, bound, shards=(), kind=jnp.bfloat16):
    factor_of = block_scale(key, extent, shards, -0.22, 0.18) if shards else 1.0
    values = jax.random.normal(key, extent, jnp.float32) * width * factor_of
    return jnp.minimum(jnp.maximum(values, -bound), bound).astype(kind)


def setup_inputs(seed: int = 0) -> dict:
    splits = jax.random.split(jax.random.key(seed), 11)
    return {
        "queries": draw_queries(jax.random.fold_in(splits[10], 71), 0),
        "keys": draw_keys(jax.random.fold_in(splits[10], 71), 0),
        "values": noise(splits[2], (BRANCHES, TOKENS, MODEL_WIDTH), 1.0, 6.0, ((0, 2), (1, 128))),
        "output_weight_matrix": noise(splits[3], (MODEL_WIDTH, MODEL_WIDTH), MODEL_WIDTH ** -0.5, 0.078125, ((0, 128),)),
        "style_down_maps": noise(splits[4], (STYLE_ADAPTERS, MODEL_WIDTH, ADAPTER_RANK), MODEL_WIDTH ** -0.5, 0.078125, ((1, 128),)),
        "style_up_maps": noise(splits[5], (STYLE_ADAPTERS, ADAPTER_RANK, MODEL_WIDTH), ADAPTER_RANK ** -0.5, 0.75),
        "branch_adapter": place_ends(jax.random.randint(splits[6], (BRANCHES,), 0, STYLE_ADAPTERS), jax.random.fold_in(splits[6], 1), 0, STYLE_ADAPTERS - 1).astype(jnp.int32),
        "guidance_weight_eighths": place_ends(jax.random.randint(splits[7], (BRANCHES,), -8, 25), jax.random.fold_in(splits[7], 1), -8, 24).astype(jnp.int32),
        "gate_offset_learned": noise(splits[8], (MODEL_WIDTH,), 0.5, 3.0, ((0, 2),), jnp.float32),
        "timestep": jax.random.randint(splits[9], (1,), 0, 1000).astype(jnp.int32),
    }


guide_unit = 0.125


def time_gate(gate_offset_learned, timestep):
    half_width = MODEL_WIDTH // 2
    columns = jnp.arange(MODEL_WIDTH, dtype=jnp.int32)
    frequency = jnp.exp((columns % half_width).astype(jnp.float32) * (-math.log(10000.0) / half_width))
    angles = timestep.astype(jnp.float32)[0] * frequency
    return gate_offset_learned + jnp.where(columns < half_width, jnp.cos(angles), jnp.sin(angles))


def attend_one(operands):
    query_rows, key_rows, value_rows = operands
    scores = jnp.dot(query_rows, key_rows.T, preferred_element_type=jnp.float32) * (HEAD_DIM ** -0.5)
    row_max = jnp.max(scores, axis=1, keepdims=True)
    weights = jnp.exp(scores - row_max)
    row_sum = jnp.sum(weights, axis=1, keepdims=True)
    mixed = jnp.dot(weights.astype(jnp.bfloat16), value_rows, preferred_element_type=jnp.float32)
    return (mixed / row_sum).astype(jnp.bfloat16)


def split_heads(tensor):
    return tensor.reshape(BRANCHES, TOKENS, HEADS, HEAD_DIM).transpose(0, 2, 1, 3).reshape(BRANCHES * HEADS, TOKENS, HEAD_DIM)


def reference(queries, keys, values, output_weight_matrix, style_down_maps, style_up_maps, branch_adapter, guidance_weight_eighths, gate_offset_learned, timestep):
    attended = lax.map(attend_one, (split_heads(queries), split_heads(keys), split_heads(values)))
    attended = attended.reshape(BRANCHES, HEADS, TOKENS, HEAD_DIM).transpose(0, 2, 1, 3).reshape(BRANCHES, TOKENS, MODEL_WIDTH)
    chosen_down_map = style_down_maps[branch_adapter]
    chosen_up_map = style_up_maps[branch_adapter]
    group_width = MODEL_WIDTH // UDEG

    def group_term(running, group_index):
        start = group_index * group_width
        columns = lax.dynamic_slice_in_dim(attended, start, group_width, 2)
        rows_here = lax.dynamic_slice_in_dim(output_weight_matrix, start, group_width, 0)
        downs = lax.dynamic_slice_in_dim(chosen_down_map, start, group_width, 1)
        plain_output = jnp.dot(columns.reshape(BRANCHES * TOKENS, group_width), rows_here, preferred_element_type=jnp.float32).reshape(BRANCHES, TOKENS, MODEL_WIDTH)
        reduced_features = jnp.einsum("btc,bcr->btr", columns.astype(jnp.float32), downs.astype(jnp.float32)).astype(jnp.bfloat16)
        adapter_out = jnp.einsum("btr,brd->btd", reduced_features.astype(jnp.float32), chosen_up_map.astype(jnp.float32))
        partial_value = lax.optimization_barrier((plain_output + adapter_out).astype(jnp.bfloat16))
        return running + partial_value.astype(jnp.float32), None

    combined, _ = lax.scan(group_term, jnp.zeros((BRANCHES, TOKENS, MODEL_WIDTH), jnp.float32), jnp.arange(UDEG, dtype=jnp.int32))
    branch_weights = guidance_weight_eighths.astype(jnp.float32) * guide_unit
    mixture = jnp.einsum("b,btd->td", branch_weights, combined)
    return (mixture * time_gate(gate_offset_learned, timestep)[None, :]).astype(jnp.bfloat16)
```

```python
import math

import jax
import jax.numpy as jnp
from jax import lax
from jax.experimental import pallas as pl
from jax.experimental.pallas import tpu as pltpu
from jax.sharding import PartitionSpec as P

MESH = pl.DeviceIdType.MESH
BF16 = jnp.bfloat16
F32 = jnp.float32
HEAD_DIM = 128
GUIDE_UNIT = 0.125
SCORE_SCALE = HEAD_DIM**-0.5 * math.log2(math.e)


def seq_of(y, x, zh, c):
    return ((y * 4 + x) * 4 + zh) * 2 + c


def wait_for(ref, sem):
    pltpu.make_async_copy(ref, ref, sem).wait()


def send(src, dst, send_sem, recv_sem, zl, s):
    return pltpu.make_async_remote_copy(
        src_ref=src, dst_ref=dst, send_sem=send_sem, recv_sem=recv_sem, device_id=(zl, s), device_id_type=MESH
    )


def body(
    adapter,
    weight_eighths,
    q_in,
    k_in,
    v_in,
    w_in,
    down_in,
    up_in,
    out,
    q_st,
    kv_st,
    w_v,
    w_sib,
    w_st,
    w_buf,
    down_v,
    down_sib,
    down_all,
    up_v,
    up_cat,
    q_buf,
    kv,
    o_t,
    m1,
    mx,
    m2,
    lr,
    lr_got,
    lr_sum,
    p_out,
    p_got,
    lr_fin,
    in_sem,
    send_sem,
    recv_sem,
    token,
):
    s = lax.axis_index("seq")
    zl = lax.axis_index("branch")
    c = s % 2
    chip = s // 2
    zh = chip % 4
    x = (chip // 4) % 4
    y = chip // 16
    col = chip // 4
    sib = s + 1 - 2 * c
    slot_left = (y // 2) * 8 + zh * 2 + y % 2
    slot = (y // 2) * 32 + x * 8 + zh * 2 + y % 2
    (
        R_SIBW,
        R_LEFT,
        R_LEFTQ,
        R_KV,
        R_Q,
        R_AG,
        R_AGSIB,
        R_KVSIB,
        R_W,
        R_WSIB,
        R_M1,
        R_M2,
        R_LR,
        R_P,
        R_LRF,
        R_SIBD,
    ) = range(16)

    def rs(i):
        return recv_sem.at[i]

    def ss(i):
        return send_sem.at[i]

    loads = [
        pltpu.make_async_copy(w_in, w_v, in_sem.at[0]),
        pltpu.make_async_copy(down_in, down_v, in_sem.at[1]),
        pltpu.make_async_copy(k_in, kv_st.at[0], in_sem.at[2]),
        pltpu.make_async_copy(v_in, kv_st.at[1], in_sem.at[3]),
        pltpu.make_async_copy(q_in, q_st, in_sem.at[4]),
        pltpu.make_async_copy(up_in.at[:, :, pl.ds(pl.multiple_of(zl * 2560, 2560), 2560)], up_v, in_sem.at[5]),
    ]
    for load in loads:
        load.start()

    barrier = pltpu.get_barrier_semaphore()

    @pl.loop(1, 64)
    def _(i):
        pl.semaphore_signal(barrier, 1, device_id=(zl, ((chip + i) % 64) * 2 + c), device_id_type=MESH)

    pl.semaphore_signal(barrier, 1, device_id=(zl, sib), device_id_type=MESH)
    pl.semaphore_signal(barrier, 1, device_id=(1 - zl, s), device_id_type=MESH)
    for load in loads[:5]:
        load.wait()
    pl.semaphore_wait(barrier, 65)

    sib_copies = [
        send(
            w_v.at[:, pl.ds(pl.multiple_of(1280 * i + 640 * (1 - c), 128), 640)],
            w_sib.at[i],
            ss(R_SIBW),
            rs(R_SIBW),
            zl,
            sib,
        )
        for i in range(4)
    ]
    sib_copies.append(send(down_v, down_sib, ss(R_SIBD), rs(R_SIBD), zl, sib))
    for copy in sib_copies:
        copy.start()

    def left_copy(i):
        y2 = i // 4
        z2 = i % 4
        head = 5 * (2 * y2 + z2 // 2) + 2
        lanes = pl.ds(pl.multiple_of(head * 128, 128), 128)
        pair = z2 % 2
        return (
            (kv_st.at[:, pair, :, lanes], kv.at[1, 0, :, x * 16 + slot_left], R_LEFT),
            (q_st.at[pair, :, lanes], q_buf.at[64 + slot_left], R_LEFTQ),
        )

    @pl.loop(1, 16)
    def _(j):
        i = (y * 4 + zh + j) % 16
        for src, dst, n in left_copy(i):
            send(src, dst, ss(n), rs(n), zl, seq_of(i // 4, x, i % 4, c)).start()

    for src, dst, n in left_copy(y * 4 + zh):
        pltpu.make_async_copy(src, dst, rs(n)).start()

    def main_copy(i):
        y2 = i // 16
        x2 = (i // 4) % 4
        z2 = i % 4
        head = 5 * (2 * y2 + x2 // 2) + 3 * (x2 % 2) + z2 // 2
        lanes = pl.ds(pl.multiple_of(head * 128, 128), 128)
        pair = z2 % 2
        return (
            (kv_st.at[:, pair, :, lanes], kv.at[0, 0, :, slot], R_KV),
            (q_st.at[pair, :, lanes], q_buf.at[slot], R_Q),
        )

    for part in range(2):

        @pl.loop(1, 64)
        def _(j):
            i = (chip + j) % 64
            src, dst, n = main_copy(i)[part]
            send(src, dst, ss(n), rs(n), zl, i * 2 + c).start()

        src, dst, n = main_copy(chip)[part]
        pltpu.make_async_copy(src, dst, rs(n)).start()

    wait_for(w_sib, rs(R_SIBW))
    wait_for(down_sib, rs(R_SIBD))
    pl.semaphore_signal(token, 1, device_id=(1 - zl, s), device_id_type=MESH)

    def joined(own, other):
        first = jnp.where(c == 0, own, other)
        second = jnp.where(c == 0, other, own)
        return jnp.concatenate([first, second], axis=0).astype(BF16)

    for i in range(4):
        own = w_v[:, pl.ds(pl.multiple_of(1280 * i + 640 * c, 128), 640)].astype(F32)
        w_st[i] = joined(own, w_sib[i].astype(F32))

    def w_copy(i):
        return w_st.at[i % 4], w_buf.at[c, col]

    @pl.loop(1, 16)
    def _(j):
        i = (col + j) % 16
        src, dst = w_copy(i)
        send(src, dst, ss(R_W), rs(R_W), zl, seq_of(i // 4, i % 4, zh, c)).start()

    src, dst = w_copy(col)
    pltpu.make_async_copy(src, dst, rs(R_W)).start()
    for i in range(4):
        down_all[i] = joined(down_v[i].astype(F32), down_sib[i].astype(F32))
    loads[5].wait()
    for i in range(4):
        up_cat[64 * i : 64 * (i + 1), :] = up_v[adapter[i]]

    slab = kv.at[1, 0, :, pl.ds(x * 16, 16)]
    wait_for(slab, rs(R_LEFT))
    wait_for(q_buf.at[pl.ds(64, 16)], rs(R_LEFTQ))

    def ag_copy(j):
        return send(slab, slab, ss(R_AG), rs(R_AG), zl, seq_of(y, (x + j) % 4, zh, c))

    for j in range(1, 4):
        ag_copy(j).start()
    wait_for(kv.at[1, 0, :, pl.ds(0, 48)], rs(R_AG))
    ag_sib = send(kv.at[1, 0], kv.at[1, 1], ss(R_AGSIB), rs(R_AGSIB), zl, sib)
    ag_sib.start()
    wait_for(kv.at[0, 0], rs(R_KV))
    kv_sib = send(kv.at[0, 0], kv.at[0, 1], ss(R_KVSIB), rs(R_KVSIB), zl, sib)
    kv_sib.start()
    wait_for(q_buf.at[pl.ds(0, 64)], rs(R_Q))
    wait_for(kv.at[1, 1], rs(R_AGSIB))
    wait_for(kv.at[0, 1], rs(R_KVSIB))

    def attend(tile, which):
        q = q_buf[pl.ds(tile * 16, 16)].reshape(256, 128)
        scores = [
            lax.dot_general(
                q, kv[which, half, 0].reshape(1024, 128), (((1,), (1,)), ((), ())), preferred_element_type=F32
            )
            * SCORE_SCALE
            for half in range(2)
        ]
        top = jnp.maximum(
            jnp.max(scores[0], axis=1, keepdims=True), jnp.max(scores[1], axis=1, keepdims=True)
        )
        total = 0.0
        mixed = 0.0
        for half in range(2):
            weights = jnp.exp2(scores[half] - top)
            total = total + jnp.sum(weights, axis=1, keepdims=True)
            mixed = mixed + jnp.dot(
                weights.astype(BF16), kv[which, half, 1].reshape(1024, 128), preferred_element_type=F32
            )
        o_t[:, pl.ds(pl.multiple_of(tile * 256, 256), 256)] = jnp.transpose(mixed / total).astype(BF16)

    unit0 = 12 * (x % 2) * (zh // 2) + 4 * (x % 2) * (1 - zh // 2) + 8 * (1 - x % 2) * (zh // 2)
    pair_all = 2 * zl + zh % 2

    def m1_copy(i):
        u = i % 8
        core2 = i // 8
        place = unit0 + u
        z2 = place // 5
        row = pl.multiple_of((place % 5) * 16, 16)
        src = o_t.at[pl.ds(pl.multiple_of(u * 16, 16), 16), pl.ds(pl.multiple_of(core2 * 512, 512), 512)]
        dst = m1.at[pair_all, pl.ds(row, 16)]
        return src, dst, z2, core2

    def m1_left_copy(i):
        odd = i % 2
        core2 = i // 2
        src = o_t.at[
            pl.ds(pl.multiple_of(odd * 64, 16), 64), pl.ds(pl.multiple_of(1024 + core2 * 128, 128), 128)
        ]
        dst = m1.at[
            pair_all, pl.ds(pl.multiple_of(16 * (1 - odd), 16), 64), pl.ds(pl.multiple_of(x * 128, 128), 128)
        ]
        return src, dst, 2 * (zh // 2) + odd, 3 * (1 - odd), core2

    def m1_start(i):
        src, dst, z2, core2 = m1_copy(i)
        mine = jnp.logical_and(jnp.logical_and(z2 == zh, c == zl), core2 == c)

        @pl.when(mine)
        def _():
            pltpu.make_async_copy(src, dst, rs(R_M1)).start()

        @pl.when(jnp.logical_not(mine))
        def _():
            send(src, dst, ss(R_M1), rs(R_M1), c, seq_of(y, x, z2, core2)).start()

    def m1_wait_send(i):
        src, dst, z2, core2 = m1_copy(i)
        mine = jnp.logical_and(jnp.logical_and(z2 == zh, c == zl), core2 == c)

        @pl.when(jnp.logical_not(mine))
        def _():
            send(src, dst, ss(R_M1), rs(R_M1), c, seq_of(y, x, z2, core2)).wait_send()

    def left_mine(x2, z2, core2):
        here = jnp.logical_and(x2 == x, z2 == zh)
        return jnp.logical_and(here, jnp.logical_and(c == zl, core2 == c))

    def m1_left_start(i):
        src, dst, x2, z2, core2 = m1_left_copy(i)
        mine = left_mine(x2, z2, core2)

        @pl.when(mine)
        def _():
            pltpu.make_async_copy(src, dst, rs(R_M1)).start()

        @pl.when(jnp.logical_not(mine))
        def _():
            send(src, dst, ss(R_M1), rs(R_M1), c, seq_of(y, x2, z2, core2)).start()

    def m1_left_wait_send(i):
        src, dst, x2, z2, core2 = m1_left_copy(i)

        @pl.when(jnp.logical_not(left_mine(x2, z2, core2)))
        def _():
            send(src, dst, ss(R_M1), rs(R_M1), c, seq_of(y, x2, z2, core2)).wait_send()

    pl.semaphore_wait(token, 1)

    @pl.loop(0, 2)
    def _(core2):
        @pl.loop(0, 2)
        def _(j):
            attend(core2 * 2 + j, 0)

        @pl.loop(0, 8)
        def _(u):
            m1_start(core2 * 8 + u)

    attend(4, 1)

    @pl.loop(0, 4)
    def _(i):
        m1_left_start(i)

    wait_for(w_buf.at[0], rs(R_W))
    w_fwd = send(w_buf.at[c], w_buf.at[c], ss(R_WSIB), rs(R_WSIB), zl, sib)
    w_fwd.start()

    wait_for(m1, rs(R_M1))
    guide = [weight_eighths[i].astype(F32) * GUIDE_UNIT for i in range(4)]
    total = m1[0].astype(F32) * guide[0]
    for i in range(1, 4):
        total = total + m1[i].astype(F32) * guide[i]
    mx[...] = total.astype(BF16)

    def m2_copy(i):
        src = mx.at[:, pl.ds(pl.multiple_of((i // 4) * 128, 128), 128)]
        return src, m2.at[col]

    @pl.loop(1, 16)
    def _(j):
        i = (col + j) % 16
        src, dst = m2_copy(i)
        send(src, dst, ss(R_M2), rs(R_M2), zl, seq_of(i // 4, i % 4, zh, c)).start()

    src, dst = m2_copy(col)
    pltpu.make_async_copy(src, dst, rs(R_M2)).start()

    ranks = jnp.concatenate(
        [
            lax.dot_general(
                down_all[adapter[i]], m1[i], (((0,), (0,)), ((), ())), preferred_element_type=F32
            )
            * guide[i]
            for i in range(4)
        ],
        axis=0,
    )
    lr[...] = jnp.transpose(ranks).astype(BF16)

    def lr_copy(i):
        src = lr.at[pl.ds(pl.multiple_of(i * 32, 32), 32)]
        return src, lr_got.at[col]

    @pl.loop(1, 16)
    def _(j):
        i = (col + j) % 16
        src, dst = lr_copy(i)
        send(src, dst, ss(R_LR), rs(R_LR), zl, seq_of(i // 4, i % 4, zh, c)).start()

    src, dst = lr_copy(col)
    pltpu.make_async_copy(src, dst, rs(R_LR)).start()

    wait_for(w_buf.at[0], rs(R_WSIB))
    wait_for(m2, rs(R_M2))
    rows = jnp.transpose(m2[...].reshape(1280, 128).astype(F32)).astype(BF16)
    for half in range(2):
        p_out[:, 640 * half : 640 * (half + 1)] = jnp.dot(
            rows, w_buf[half].reshape(1280, 640), preferred_element_type=F32
        ).astype(BF16)

    def p_copy(i):
        z2 = i // 2
        y2 = 2 * c + i % 2
        src = p_out.at[pl.ds(pl.multiple_of(i * 16, 16), 16)]
        dst = p_got.at[zh, :, pl.ds(pl.multiple_of((x % 2) * 1280, 1280), 1280)]
        here = jnp.logical_and(jnp.logical_and(y2 == y, y == x), jnp.logical_and(z2 == zh, x // 2 == zl))
        return src, dst, seq_of(y2, y, z2, zl), jnp.logical_and(here, c == zl)

    @pl.loop(0, 8)
    def _(i):
        src, dst, to, mine = p_copy(i)

        @pl.when(mine)
        def _():
            pltpu.make_async_copy(src, dst, rs(R_P)).start()

        @pl.when(jnp.logical_not(mine))
        def _():
            send(src, dst, ss(R_P), rs(R_P), x // 2, to).start()

    wait_for(lr_got, rs(R_LR))
    low = lr_got[0].astype(F32)
    for i in range(1, 16):
        low = low + lr_got[i].astype(F32)
    lr_sum[...] = low.astype(BF16)

    def lrf_copy(i):
        y2 = 2 * c + i // 2
        zl2 = i % 2
        src = lr_sum.at[pl.ds(pl.multiple_of((i // 2) * 16, 16), 16)]
        dst = lr_fin.at[zh]
        here = jnp.logical_and(jnp.logical_and(y2 == y, y == x), jnp.logical_and(x == zh, zl2 == zl))
        return src, dst, zl2, seq_of(y2, y, x, zl), jnp.logical_and(here, c == zl)

    @pl.loop(0, 4)
    def _(i):
        src, dst, zl2, to, mine = lrf_copy(i)

        @pl.when(mine)
        def _():
            pltpu.make_async_copy(src, dst, rs(R_LRF)).start()

        @pl.when(jnp.logical_not(mine))
        def _():
            send(src, dst, ss(R_LRF), rs(R_LRF), zl2, to).start()

    wait_for(lr_fin, rs(R_LRF))
    low = lr_fin[0].astype(F32)
    for i in range(1, 4):
        low = low + lr_fin[i].astype(F32)
    adapted = jnp.dot(low.astype(BF16), up_cat[...], preferred_element_type=F32)
    wait_for(p_got, rs(R_P))
    for i in range(4):
        adapted = adapted + p_got[i].astype(F32)
    out[...] = adapted

    for copy in sib_copies:
        copy.wait_send()
    wait_for(kv.at[1, 0, :, pl.ds(0, 15)], ss(R_LEFT))
    wait_for(q_buf.at[pl.ds(0, 15)], ss(R_LEFTQ))
    wait_for(kv.at[0, 0, :, pl.ds(0, 63)], ss(R_KV))
    wait_for(q_buf.at[pl.ds(0, 63)], ss(R_Q))
    wait_for(w_buf.at[0, pl.ds(0, 15)], ss(R_W))
    wait_for(kv.at[1, 0, :, pl.ds(0, 48)], ss(R_AG))
    ag_sib.wait_send()
    kv_sib.wait_send()
    w_fwd.wait_send()

    @pl.loop(0, 16)
    def _(i):
        m1_wait_send(i)

    @pl.loop(0, 4)
    def _(i):
        m1_left_wait_send(i)

    wait_for(m2.at[pl.ds(0, 15)], ss(R_M2))
    wait_for(lr_got.at[pl.ds(0, 15)], ss(R_LR))

    @pl.loop(0, 8)
    def _(i):
        src, dst, to, mine = p_copy(i)

        @pl.when(jnp.logical_not(mine))
        def _():
            send(src, dst, ss(R_P), rs(R_P), x // 2, to).wait_send()

    @pl.loop(0, 4)
    def _(i):
        src, dst, zl2, to, mine = lrf_copy(i)

        @pl.when(jnp.logical_not(mine))
        def _():
            send(src, dst, ss(R_LRF), rs(R_LRF), zl2, to).wait_send()


def shards(q, k, v, w, down, up, adapter, weight_eighths, gate_offset, timestep):
    whole = pl.BlockSpec(memory_space=pl.ANY)
    smem = pl.BlockSpec(memory_space=pltpu.SMEM)
    vm = pltpu.VMEM
    mixture = pl.pallas_call(
        body,
        out_shape=jax.ShapeDtypeStruct((16, 2560), F32),
        in_specs=[smem, smem] + [whole] * 6,
        out_specs=pl.BlockSpec(memory_space=pltpu.VMEM),
        scratch_shapes=[
            vm((2, 16, 5120), BF16),
            vm((2, 2, 16, 5120), BF16),
            vm((40, 5120), BF16),
            vm((4, 40, 640), BF16),
            vm((4, 80, 640), BF16),
            vm((2, 16, 80, 640), BF16),
            vm((4, 40, 64), BF16),
            vm((4, 40, 64), BF16),
            vm((4, 80, 64), BF16),
            vm((4, 64, 2560), BF16),
            vm((256, 2560), BF16),
            vm((80, 16, 128), BF16),
            vm((2, 2, 2, 64, 16, 128), BF16),
            vm((128, 1280), BF16),
            vm((4, 80, 512), BF16),
            vm((80, 512), BF16),
            vm((16, 80, 128), BF16),
            vm((512, 256), BF16),
            vm((16, 32, 256), BF16),
            vm((32, 256), BF16),
            vm((128, 1280), BF16),
            vm((4, 16, 2560), BF16),
            vm((4, 16, 256), BF16),
            pltpu.SemaphoreType.DMA((6,)),
            pltpu.SemaphoreType.DMA((16,)),
            pltpu.SemaphoreType.DMA((16,)),
            pltpu.SemaphoreType.REGULAR,
        ],
        compiler_params=pltpu.CompilerParams(
            collective_id=0, has_side_effects=True, vmem_limit_bytes=48 * 2**20
        ),
        name="guided_attention",
    )(adapter, weight_eighths, q, k, v, w, down, up)

    columns = lax.axis_index("branch") * 2560 + jnp.arange(2560, dtype=jnp.int32)
    frequency = jnp.exp((columns % 2560).astype(F32) * (-math.log(10000.0) / 2560))
    angles = timestep.astype(F32)[0] * frequency
    gate_row = gate_offset + jnp.where(columns < 2560, jnp.cos(angles), jnp.sin(angles))
    return (mixture * gate_row[None, :]).astype(BF16)


def solution(mesh):
    placed = (
        P("branch", "seq", None),
        P("branch", "seq", None),
        P("branch", "seq", None),
        P("seq", None),
        P(None, "seq", None),
        P(),
        P(),
        P(),
        P("branch"),
        P(),
    )
    return jax.shard_map(
        shards, mesh=mesh, in_specs=placed, out_specs=P("seq", "branch"), check_vma=False
    )
```

```python
import math

import jax
import jax.numpy as jnp
from jax import lax
from jax.experimental import pallas as pl
from jax.experimental.pallas import tpu as pltpu
from jax.sharding import PartitionSpec as P

MESH = pl.DeviceIdType.MESH
BF16 = jnp.bfloat16
F32 = jnp.float32
HEAD_DIM = 128
GUIDE_UNIT = 0.125
SCORE_SCALE = HEAD_DIM**-0.5 * math.log2(math.e)


def seq_of(y, x, zh, c):
    return ((y * 4 + x) * 4 + zh) * 2 + c


def wait_for(ref, sem):
    pltpu.make_async_copy(ref, ref, sem).wait()


def send(src, dst, send_sem, recv_sem, zl, s):
    return pltpu.make_async_remote_copy(
        src_ref=src, dst_ref=dst, send_sem=send_sem, recv_sem=recv_sem, device_id=(zl, s), device_id_type=MESH
    )


def body(
    adapter,
    weight_eighths,
    q_in,
    k_in,
    v_in,
    w_in,
    down_in,
    up_in,
    out,
    q_st,
    kv_st,
    w_v,
    w_sib,
    w_st,
    w_buf,
    down_v,
    down_sib,
    down_all,
    up_v,
    up_cat,
    q_buf,
    kv,
    o_t,
    m1,
    mx,
    m2,
    lr,
    lr_got,
    lr_sum,
    p_out,
    p_got,
    lr_fin,
    in_sem,
    send_sem,
    recv_sem,
    token,
):
    s = lax.axis_index("seq")
    zl = lax.axis_index("branch")
    c = s % 2
    chip = s // 2
    zh = chip % 4
    x = (chip // 4) % 4
    y = chip // 16
    col = chip // 4
    sib = s + 1 - 2 * c
    slot_left = (x // 2) * 8 + (x % 2) * 4 + zh
    slot = (x // 2) * 32 + y * 8 + (x % 2) * 4 + zh
    (
        R_SIBW,
        R_LEFT,
        R_LEFTQ,
        R_KV,
        R_Q,
        R_AG,
        R_AGSIB,
        R_KVSIB,
        R_W,
        R_WSIB,
        R_M1,
        R_M2,
        R_LR,
        R_P,
        R_LRF,
        R_SIBD,
        R_WX,
    ) = range(17)

    def rs(i):
        return recv_sem.at[i]

    def ss(i):
        return send_sem.at[i]

    loads = [
        pltpu.make_async_copy(w_in, w_v, in_sem.at[0]),
        pltpu.make_async_copy(down_in, down_v, in_sem.at[1]),
        pltpu.make_async_copy(k_in, kv_st.at[0], in_sem.at[2]),
        pltpu.make_async_copy(v_in, kv_st.at[1], in_sem.at[3]),
        pltpu.make_async_copy(q_in, q_st, in_sem.at[4]),
        pltpu.make_async_copy(up_in.at[:, :, pl.ds(pl.multiple_of(zl * 2560, 2560), 2560)], up_v, in_sem.at[5]),
    ]
    for load in loads:
        load.start()

    barrier = pltpu.get_barrier_semaphore()

    @pl.loop(1, 64)
    def _(i):
        pl.semaphore_signal(barrier, 1, device_id=(zl, ((chip + i) % 64) * 2 + c), device_id_type=MESH)

    pl.semaphore_signal(barrier, 1, device_id=(zl, sib), device_id_type=MESH)
    pl.semaphore_signal(barrier, 1, device_id=(1 - zl, s), device_id_type=MESH)
    for load in loads[:5]:
        load.wait()
    pl.semaphore_wait(barrier, 65)

    sib_copies = [
        send(
            w_v.at[:, pl.ds(pl.multiple_of(1280 * i + 640 * (1 - c), 128), 640)],
            w_sib.at[i],
            ss(R_SIBW),
            rs(R_SIBW),
            zl,
            sib,
        )
        for i in range(4)
    ]
    sib_copies.append(send(down_v, down_sib, ss(R_SIBD), rs(R_SIBD), zl, sib))
    for copy in sib_copies:
        copy.start()

    wait_for(w_sib, rs(R_SIBW))
    wait_for(down_sib, rs(R_SIBD))
    pl.semaphore_signal(token, 1, device_id=(1 - zl, s), device_id_type=MESH)

    def joined(own, other):
        first = jnp.where(c == 0, own, other)
        second = jnp.where(c == 0, other, own)
        return jnp.concatenate([first, second], axis=0).astype(BF16)

    for i in range(4):
        own = w_v[:, pl.ds(pl.multiple_of(1280 * i + 640 * c, 128), 640)].astype(F32)
        w_st[i] = joined(own, w_sib[i].astype(F32))
    for j in range(1, 4):
        i = (x + j) % 4
        send(w_st.at[i], w_buf.at[c, col], ss(R_WX), rs(R_WX), zl, seq_of(y, i, zh, c)).start()
    pltpu.make_async_copy(w_st.at[x], w_buf.at[c, col], rs(R_WX)).start()

    def left_copy(i):
        y2 = i // 4
        z2 = i % 4
        head = 5 * (2 * y2 + z2 // 2) + 2
        lanes = pl.ds(pl.multiple_of(head * 128, 128), 128)
        pair = z2 % 2
        return (
            (kv_st.at[:, pair, :, lanes], kv.at[1, 0, :, x * 16 + y * 4 + zh], R_LEFT),
            (q_st.at[pair, :, lanes], q_buf.at[64 + slot_left], R_LEFTQ),
        )

    @pl.loop(1, 16)
    def _(j):
        i = (y * 4 + zh + j) % 16
        (src, dst, n), (src_q, dst_q, n_q) = left_copy(i)
        send(src, dst, ss(n), rs(n), zl, seq_of(i // 4, x, i % 4, c)).start()
        send(src_q, dst_q, ss(n_q), rs(n_q), zl, seq_of(i // 4, y, i % 4, c)).start()

    (src, dst, n), (src_q, dst_q, n_q) = left_copy(y * 4 + zh)
    pltpu.make_async_copy(src, dst, rs(n)).start()
    left_q_far = send(src_q, dst_q, ss(n_q), rs(n_q), zl, seq_of(y, y, zh, c))

    @pl.when(x == y)
    def _():
        pltpu.make_async_copy(src_q, dst_q, rs(n_q)).start()

    @pl.when(x != y)
    def _():
        left_q_far.start()

    def main_copy(i):
        y2 = i // 16
        x2 = (i // 4) % 4
        z2 = i % 4
        head = 5 * (2 * y2 + x2 // 2) + 3 * (x2 % 2) + z2 // 2
        lanes = pl.ds(pl.multiple_of(head * 128, 128), 128)
        pair = z2 % 2
        return (
            (kv_st.at[:, pair, :, lanes], kv.at[0, 0, :, slot], R_KV),
            (q_st.at[pair, :, lanes], q_buf.at[slot], R_Q),
        )

    def main_sends(part):
        @pl.loop(1, 64)
        def _(j):
            i = (chip + j) % 64
            src, dst, n = main_copy(i)[part]
            send(src, dst, ss(n), rs(n), zl, i * 2 + c).start()

        src, dst, n = main_copy(chip)[part]
        pltpu.make_async_copy(src, dst, rs(n)).start()

    main_sends(0)
    w_slab = w_buf.at[c, pl.ds(y * 4, 4)]
    wait_for(w_slab, rs(R_WX))
    for j in range(1, 4):
        send(w_slab, w_slab, ss(R_W), rs(R_W), zl, seq_of((y + j) % 4, x, zh, c)).start()
    main_sends(1)
    for i in range(4):
        down_all[i] = joined(down_v[i].astype(F32), down_sib[i].astype(F32))
    loads[5].wait()
    for i in range(4):
        up_cat[64 * i : 64 * (i + 1), :] = up_v[adapter[i]]

    slab = kv.at[1, 0, :, pl.ds(x * 16, 16)]
    wait_for(slab, rs(R_LEFT))
    wait_for(q_buf.at[pl.ds(64, 16)], rs(R_LEFTQ))

    def ag_copy(j):
        return send(slab, slab, ss(R_AG), rs(R_AG), zl, seq_of(y, (x + j) % 4, zh, c))

    for j in range(1, 4):
        ag_copy(j).start()
    wait_for(kv.at[1, 0, :, pl.ds(0, 48)], rs(R_AG))
    ag_sib = send(kv.at[1, 0], kv.at[1, 1], ss(R_AGSIB), rs(R_AGSIB), zl, sib)
    ag_sib.start()
    wait_for(kv.at[0, 0], rs(R_KV))
    kv_sib = send(kv.at[0, 0], kv.at[0, 1], ss(R_KVSIB), rs(R_KVSIB), zl, sib)
    kv_sib.start()
    wait_for(q_buf.at[pl.ds(0, 64)], rs(R_Q))
    wait_for(kv.at[1, 1], rs(R_AGSIB))
    wait_for(kv.at[0, 1], rs(R_KVSIB))

    def attend(tile, which):
        q = q_buf[pl.ds(tile * 16, 16)].reshape(256, 128)
        scores = [
            lax.dot_general(
                q, kv[which, half, 0].reshape(1024, 128), (((1,), (1,)), ((), ())), preferred_element_type=F32
            )
            * SCORE_SCALE
            for half in range(2)
        ]
        top = jnp.maximum(
            jnp.max(scores[0], axis=1, keepdims=True), jnp.max(scores[1], axis=1, keepdims=True)
        )
        total = 0.0
        mixed = 0.0
        for half in range(2):
            weights = jnp.exp2(scores[half] - top)
            total = total + jnp.sum(weights, axis=1, keepdims=True)
            mixed = mixed + jnp.dot(
                weights.astype(BF16), kv[which, half, 1].reshape(1024, 128), preferred_element_type=F32
            )
        o_t[:, pl.ds(pl.multiple_of(tile * 256, 256), 256)] = jnp.transpose(mixed / total).astype(BF16)

    unit0 = 12 * (x % 2) * (zh // 2) + 4 * (x % 2) * (1 - zh // 2) + 8 * (1 - x % 2) * (zh // 2)
    pair_all = 2 * zl + zh % 2

    def m1_copy(i):
        u = i % 8
        core2 = i // 8
        place = unit0 + u
        z2 = place // 5
        row = pl.multiple_of((place % 5) * 16, 16)
        src = o_t.at[pl.ds(pl.multiple_of(u * 16, 16), 16), pl.ds(pl.multiple_of(core2 * 512, 512), 512)]
        dst = m1.at[pair_all, pl.ds(row, 16)]
        return src, dst, z2, core2

    def m1_left_copy(i):
        odd = i % 2
        core2 = i // 2
        src = o_t.at[
            pl.ds(pl.multiple_of(odd * 64, 16), 64), pl.ds(pl.multiple_of(1024 + core2 * 128, 128), 128)
        ]
        dst = m1.at[
            pair_all, pl.ds(pl.multiple_of(16 * (1 - odd), 16), 64), pl.ds(pl.multiple_of(x * 128, 128), 128)
        ]
        return src, dst, 2 * (zh // 2) + odd, 3 * (1 - odd), core2

    def m1_start(i):
        src, dst, z2, core2 = m1_copy(i)
        mine = jnp.logical_and(jnp.logical_and(z2 == zh, c == zl), core2 == c)

        @pl.when(mine)
        def _():
            pltpu.make_async_copy(src, dst, rs(R_M1)).start()

        @pl.when(jnp.logical_not(mine))
        def _():
            send(src, dst, ss(R_M1), rs(R_M1), c, seq_of(y, x, z2, core2)).start()

    def m1_wait_send(i):
        src, dst, z2, core2 = m1_copy(i)
        mine = jnp.logical_and(jnp.logical_and(z2 == zh, c == zl), core2 == c)

        @pl.when(jnp.logical_not(mine))
        def _():
            send(src, dst, ss(R_M1), rs(R_M1), c, seq_of(y, x, z2, core2)).wait_send()

    def left_mine(x2, z2, core2):
        here = jnp.logical_and(x2 == x, z2 == zh)
        return jnp.logical_and(here, jnp.logical_and(c == zl, core2 == c))

    def m1_left_start(i):
        src, dst, x2, z2, core2 = m1_left_copy(i)
        mine = left_mine(x2, z2, core2)

        @pl.when(mine)
        def _():
            pltpu.make_async_copy(src, dst, rs(R_M1)).start()

        @pl.when(jnp.logical_not(mine))
        def _():
            send(src, dst, ss(R_M1), rs(R_M1), c, seq_of(y, x2, z2, core2)).start()

    def m1_left_wait_send(i):
        src, dst, x2, z2, core2 = m1_left_copy(i)

        @pl.when(jnp.logical_not(left_mine(x2, z2, core2)))
        def _():
            send(src, dst, ss(R_M1), rs(R_M1), c, seq_of(y, x2, z2, core2)).wait_send()

    pl.semaphore_wait(token, 1)

    @pl.loop(0, 2)
    def _(core2):
        @pl.loop(0, 2)
        def _(j):
            attend(core2 * 2 + j, 0)

        @pl.loop(0, 8)
        def _(u):
            m1_start(core2 * 8 + u)

    attend(4, 1)

    @pl.loop(0, 4)
    def _(i):
        m1_left_start(i)

    wait_for(w_buf.at[0, pl.ds(0, 12)], rs(R_W))
    w_fwd = send(w_buf.at[c], w_buf.at[c], ss(R_WSIB), rs(R_WSIB), zl, sib)
    w_fwd.start()

    wait_for(m1, rs(R_M1))
    guide = [weight_eighths[i].astype(F32) * GUIDE_UNIT for i in range(4)]
    total = m1[0].astype(F32) * guide[0]
    for i in range(1, 4):
        total = total + m1[i].astype(F32) * guide[i]
    mx[...] = total.astype(BF16)

    def m2_copy(i):
        src = mx.at[:, pl.ds(pl.multiple_of((i // 4) * 128, 128), 128)]
        return src, m2.at[col]

    @pl.loop(1, 16)
    def _(j):
        i = (col + j) % 16
        src, dst = m2_copy(i)
        send(src, dst, ss(R_M2), rs(R_M2), zl, seq_of(i // 4, i % 4, zh, c)).start()

    src, dst = m2_copy(col)
    pltpu.make_async_copy(src, dst, rs(R_M2)).start()

    ranks = jnp.concatenate(
        [
            lax.dot_general(
                down_all[adapter[i]], m1[i], (((0,), (0,)), ((), ())), preferred_element_type=F32
            )
            * guide[i]
            for i in range(4)
        ],
        axis=0,
    )
    lr[...] = jnp.transpose(ranks).astype(BF16)

    def lr_copy(i):
        src = lr.at[pl.ds(pl.multiple_of(i * 32, 32), 32)]
        return src, lr_got.at[col]

    @pl.loop(1, 16)
    def _(j):
        i = (col + j) % 16
        src, dst = lr_copy(i)
        send(src, dst, ss(R_LR), rs(R_LR), zl, seq_of(i // 4, i % 4, zh, c)).start()

    src, dst = lr_copy(col)
    pltpu.make_async_copy(src, dst, rs(R_LR)).start()

    wait_for(w_buf.at[0], rs(R_WSIB))
    wait_for(m2, rs(R_M2))
    rows = jnp.transpose(m2[...].reshape(1280, 128).astype(F32)).astype(BF16)
    for half in range(2):
        p_out[:, 640 * half : 640 * (half + 1)] = jnp.dot(
            rows, w_buf[half].reshape(1280, 640), preferred_element_type=F32
        ).astype(BF16)

    def p_copy(i):
        x2 = 2 * c + i // 4
        z2 = i % 4
        src = p_out.at[pl.ds(pl.multiple_of(i * 16, 16), 16)]
        dst = p_got.at[zh, :, pl.ds(pl.multiple_of((x % 2) * 1280, 1280), 1280)]
        here = jnp.logical_and(jnp.logical_and(x2 == x, z2 == zh), x // 2 == zl)
        return src, dst, seq_of(y, x2, z2, zl), jnp.logical_and(here, c == zl)

    @pl.loop(0, 8)
    def _(i):
        src, dst, to, mine = p_copy(i)

        @pl.when(mine)
        def _():
            pltpu.make_async_copy(src, dst, rs(R_P)).start()

        @pl.when(jnp.logical_not(mine))
        def _():
            send(src, dst, ss(R_P), rs(R_P), x // 2, to).start()

    wait_for(lr_got, rs(R_LR))
    low = lr_got[0].astype(F32)
    for i in range(1, 16):
        low = low + lr_got[i].astype(F32)
    lr_sum[...] = low.astype(BF16)

    def lrf_copy(i):
        x2 = 2 * c + x // 2
        z2 = 2 * (x % 2) + i // 2
        zl2 = i % 2
        src = lr_sum.at[pl.ds(pl.multiple_of((i // 2) * 16, 16), 16)]
        dst = lr_fin.at[zh]
        here = jnp.logical_and(jnp.logical_and(x2 == x, z2 == zh), zl2 == zl)
        return src, dst, zl2, seq_of(y, x2, z2, zl), jnp.logical_and(here, c == zl)

    @pl.loop(0, 4)
    def _(i):
        src, dst, zl2, to, mine = lrf_copy(i)

        @pl.when(mine)
        def _():
            pltpu.make_async_copy(src, dst, rs(R_LRF)).start()

        @pl.when(jnp.logical_not(mine))
        def _():
            send(src, dst, ss(R_LRF), rs(R_LRF), zl2, to).start()

    wait_for(lr_fin, rs(R_LRF))
    low = lr_fin[0].astype(F32)
    for i in range(1, 4):
        low = low + lr_fin[i].astype(F32)
    adapted = jnp.dot(low.astype(BF16), up_cat[...], preferred_element_type=F32)
    wait_for(p_got, rs(R_P))
    for i in range(4):
        adapted = adapted + p_got[i].astype(F32)
    out[...] = adapted

    for copy in sib_copies:
        copy.wait_send()
    wait_for(kv.at[1, 0, :, pl.ds(0, 15)], ss(R_LEFT))
    wait_for(q_buf.at[pl.ds(0, 15)], ss(R_LEFTQ))

    @pl.when(x != y)
    def _():
        left_q_far.wait_send()

    wait_for(kv.at[0, 0, :, pl.ds(0, 63)], ss(R_KV))
    wait_for(q_buf.at[pl.ds(0, 63)], ss(R_Q))
    wait_for(w_buf.at[0, pl.ds(0, 3)], ss(R_WX))
    wait_for(w_buf.at[0, pl.ds(0, 12)], ss(R_W))
    wait_for(kv.at[1, 0, :, pl.ds(0, 48)], ss(R_AG))
    ag_sib.wait_send()
    kv_sib.wait_send()
    w_fwd.wait_send()

    @pl.loop(0, 16)
    def _(i):
        m1_wait_send(i)

    @pl.loop(0, 4)
    def _(i):
        m1_left_wait_send(i)

    wait_for(m2.at[pl.ds(0, 15)], ss(R_M2))
    wait_for(lr_got.at[pl.ds(0, 15)], ss(R_LR))

    @pl.loop(0, 8)
    def _(i):
        src, dst, to, mine = p_copy(i)

        @pl.when(jnp.logical_not(mine))
        def _():
            send(src, dst, ss(R_P), rs(R_P), x // 2, to).wait_send()

    @pl.loop(0, 4)
    def _(i):
        src, dst, zl2, to, mine = lrf_copy(i)

        @pl.when(jnp.logical_not(mine))
        def _():
            send(src, dst, ss(R_LRF), rs(R_LRF), zl2, to).wait_send()


def shards(q, k, v, w, down, up, adapter, weight_eighths, gate_offset, timestep):
    whole = pl.BlockSpec(memory_space=pl.ANY)
    smem = pl.BlockSpec(memory_space=pltpu.SMEM)
    vm = pltpu.VMEM
    mixture = pl.pallas_call(
        body,
        out_shape=jax.ShapeDtypeStruct((16, 2560), F32),
        in_specs=[smem, smem] + [whole] * 6,
        out_specs=pl.BlockSpec(memory_space=pltpu.VMEM),
        scratch_shapes=[
            vm((2, 16, 5120), BF16),
            vm((2, 2, 16, 5120), BF16),
            vm((40, 5120), BF16),
            vm((4, 40, 640), BF16),
            vm((4, 80, 640), BF16),
            vm((2, 16, 80, 640), BF16),
            vm((4, 40, 64), BF16),
            vm((4, 40, 64), BF16),
            vm((4, 80, 64), BF16),
            vm((4, 64, 2560), BF16),
            vm((256, 2560), BF16),
            vm((80, 16, 128), BF16),
            vm((2, 2, 2, 64, 16, 128), BF16),
            vm((128, 1280), BF16),
            vm((4, 80, 512), BF16),
            vm((80, 512), BF16),
            vm((16, 80, 128), BF16),
            vm((512, 256), BF16),
            vm((16, 32, 256), BF16),
            vm((32, 256), BF16),
            vm((128, 1280), BF16),
            vm((4, 16, 2560), BF16),
            vm((4, 16, 256), BF16),
            pltpu.SemaphoreType.DMA((6,)),
            pltpu.SemaphoreType.DMA((17,)),
            pltpu.SemaphoreType.DMA((17,)),
            pltpu.SemaphoreType.REGULAR,
        ],
        compiler_params=pltpu.CompilerParams(
            collective_id=0, has_side_effects=True, vmem_limit_bytes=62 * 2**20
        ),
        name="guided_attention",
    )(adapter, weight_eighths, q, k, v, w, down, up)

    columns = lax.axis_index("branch") * 2560 + jnp.arange(2560, dtype=jnp.int32)
    frequency = jnp.exp((columns % 2560).astype(F32) * (-math.log(10000.0) / 2560))
    angles = timestep.astype(F32)[0] * frequency
    gate_row = gate_offset + jnp.where(columns < 2560, jnp.cos(angles), jnp.sin(angles))
    return (mixture * gate_row[None, :]).astype(BF16)


def solution(mesh):
    placed = (
        P("branch", "seq", None),
        P("branch", "seq", None),
        P("branch", "seq", None),
        P("seq", None),
        P(None, "seq", None),
        P(),
        P(),
        P(),
        P("branch"),
        P(),
    )
    return jax.shard_map(
        shards, mesh=mesh, in_specs=placed, out_specs=P("seq", "branch"), check_vma=False
    )
```

```python
import math

import jax
import jax.numpy as jnp
from jax import lax
from jax.experimental import pallas as pl
from jax.experimental.pallas import tpu as pltpu
from jax.sharding import PartitionSpec as P

MESH = pl.DeviceIdType.MESH
BF16 = jnp.bfloat16
F32 = jnp.float32
HEAD_DIM = 128
GUIDE_UNIT = 0.125
SCORE_SCALE = HEAD_DIM**-0.5 * math.log2(math.e)


def seq_of(y, x, zh, c):
    return ((y * 4 + x) * 4 + zh) * 2 + c


def wait_for(ref, sem):
    pltpu.make_async_copy(ref, ref, sem).wait()


def send(src, dst, send_sem, recv_sem, zl, s):
    return pltpu.make_async_remote_copy(
        src_ref=src, dst_ref=dst, send_sem=send_sem, recv_sem=recv_sem, device_id=(zl, s), device_id_type=MESH
    )


def body(
    adapter,
    weight_eighths,
    q_in,
    k_in,
    v_in,
    w_in,
    down_in,
    up_in,
    out,
    qkv_st,
    w_v,
    w_sib,
    w_st,
    w_buf,
    down_v,
    down_sib,
    down_all,
    up_v,
    up_cat,
    main,
    main_sib,
    left_q,
    left,
    left_sib,
    o_t,
    m1,
    mx,
    m2,
    lr,
    lr_got,
    lr_sum,
    p_out,
    p_got,
    lr_fin,
    in_sem,
    send_sem,
    recv_sem,
    token,
):
    s = lax.axis_index("seq")
    zl = lax.axis_index("branch")
    c = s % 2
    chip = s // 2
    zh = chip % 4
    x = (chip // 4) % 4
    y = chip // 16
    col = chip // 4
    sib = s + 1 - 2 * c
    slot_left = (x // 2) * 8 + (x % 2) * 4 + zh
    slot = (x // 2) * 32 + y * 8 + (x % 2) * 4 + zh
    (
        R_SIBW,
        R_LEFT,
        R_LEFTQ,
        R_MAIN,
        R_AG,
        R_AGSIB,
        R_KVSIB,
        R_W,
        R_WSIB,
        R_M1,
        R_M2,
        R_LR,
        R_P,
        R_LRF,
        R_SIBD,
        R_WX,
    ) = range(16)

    def rs(i):
        return recv_sem.at[i]

    def ss(i):
        return send_sem.at[i]

    loads = [
        pltpu.make_async_copy(w_in, w_v, in_sem.at[0]),
        pltpu.make_async_copy(down_in, down_v, in_sem.at[1]),
        pltpu.make_async_copy(k_in, qkv_st.at[1], in_sem.at[2]),
        pltpu.make_async_copy(v_in, qkv_st.at[2], in_sem.at[3]),
        pltpu.make_async_copy(q_in, qkv_st.at[0], in_sem.at[4]),
        pltpu.make_async_copy(up_in.at[:, :, pl.ds(pl.multiple_of(zl * 2560, 2560), 2560)], up_v, in_sem.at[5]),
    ]
    for load in loads:
        load.start()

    barrier = pltpu.get_barrier_semaphore()

    @pl.loop(1, 64)
    def _(i):
        pl.semaphore_signal(barrier, 1, device_id=(zl, ((chip + i) % 64) * 2 + c), device_id_type=MESH)

    pl.semaphore_signal(barrier, 1, device_id=(zl, sib), device_id_type=MESH)
    pl.semaphore_signal(barrier, 1, device_id=(1 - zl, s), device_id_type=MESH)
    for load in loads[:5]:
        load.wait()
    pl.semaphore_wait(barrier, 65)

    sib_copies = [
        send(
            w_v.at[:, pl.ds(pl.multiple_of(1280 * i + 640 * (1 - c), 128), 640)],
            w_sib.at[i],
            ss(R_SIBW),
            rs(R_SIBW),
            zl,
            sib,
        )
        for i in range(4)
    ]
    sib_copies.append(send(down_v, down_sib, ss(R_SIBD), rs(R_SIBD), zl, sib))
    for copy in sib_copies:
        copy.start()

    wait_for(w_sib, rs(R_SIBW))
    wait_for(down_sib, rs(R_SIBD))
    pl.semaphore_signal(token, 1, device_id=(1 - zl, s), device_id_type=MESH)

    def joined(own, other):
        first = jnp.where(c == 0, own, other)
        second = jnp.where(c == 0, other, own)
        return jnp.concatenate([first, second], axis=0).astype(BF16)

    for i in range(4):
        own = w_v[:, pl.ds(pl.multiple_of(1280 * i + 640 * c, 128), 640)].astype(F32)
        w_st[i] = joined(own, w_sib[i].astype(F32))
    for j in range(1, 4):
        i = (x + j) % 4
        send(w_st.at[i], w_buf.at[c, col], ss(R_WX), rs(R_WX), zl, seq_of(y, i, zh, c)).start()
    pltpu.make_async_copy(w_st.at[x], w_buf.at[c, col], rs(R_WX)).start()

    def left_copy(i):
        y2 = i // 4
        z2 = i % 4
        head = 5 * (2 * y2 + z2 // 2) + 2
        lanes = pl.ds(pl.multiple_of(head * 128, 128), 128)
        pair = z2 % 2
        return (
            (qkv_st.at[pl.ds(1, 2), pair, :, lanes], left.at[:, x * 16 + y * 4 + zh], R_LEFT),
            (qkv_st.at[0, pair, :, lanes], left_q.at[slot_left], R_LEFTQ),
        )

    @pl.loop(1, 16)
    def _(j):
        i = (y * 4 + zh + j) % 16
        (src, dst, n), (src_q, dst_q, n_q) = left_copy(i)
        send(src, dst, ss(n), rs(n), zl, seq_of(i // 4, x, i % 4, c)).start()
        send(src_q, dst_q, ss(n_q), rs(n_q), zl, seq_of(i // 4, y, i % 4, c)).start()

    (src, dst, n), (src_q, dst_q, n_q) = left_copy(y * 4 + zh)
    pltpu.make_async_copy(src, dst, rs(n)).start()
    left_q_far = send(src_q, dst_q, ss(n_q), rs(n_q), zl, seq_of(y, y, zh, c))

    @pl.when(x == y)
    def _():
        pltpu.make_async_copy(src_q, dst_q, rs(n_q)).start()

    @pl.when(x != y)
    def _():
        left_q_far.start()

    def main_copy(i):
        y2 = i // 16
        x2 = (i // 4) % 4
        z2 = i % 4
        head = 5 * (2 * y2 + x2 // 2) + 3 * (x2 % 2) + z2 // 2
        lanes = pl.ds(pl.multiple_of(head * 128, 128), 128)
        pair = z2 % 2
        return qkv_st.at[:, pair, :, lanes], main.at[:, slot]

    @pl.loop(1, 64)
    def _(j):
        i = (chip + j) % 64
        src, dst = main_copy(i)
        send(src, dst, ss(R_MAIN), rs(R_MAIN), zl, i * 2 + c).start()

    src, dst = main_copy(chip)
    pltpu.make_async_copy(src, dst, rs(R_MAIN)).start()
    w_slab = w_buf.at[c, pl.ds(y * 4, 4)]
    wait_for(w_slab, rs(R_WX))
    for j in range(1, 4):
        send(w_slab, w_slab, ss(R_W), rs(R_W), zl, seq_of((y + j) % 4, x, zh, c)).start()
    for i in range(4):
        down_all[i] = joined(down_v[i].astype(F32), down_sib[i].astype(F32))
    loads[5].wait()
    for i in range(4):
        up_cat[64 * i : 64 * (i + 1), :] = up_v[adapter[i]]

    slab = left.at[:, pl.ds(x * 16, 16)]
    wait_for(slab, rs(R_LEFT))
    wait_for(left_q, rs(R_LEFTQ))

    def ag_copy(j):
        return send(slab, slab, ss(R_AG), rs(R_AG), zl, seq_of(y, (x + j) % 4, zh, c))

    for j in range(1, 4):
        ag_copy(j).start()
    wait_for(left.at[:, pl.ds(0, 48)], rs(R_AG))
    ag_sib = send(left, left_sib, ss(R_AGSIB), rs(R_AGSIB), zl, sib)
    ag_sib.start()
    wait_for(main, rs(R_MAIN))
    kv_sib = send(main.at[pl.ds(1, 2)], main_sib, ss(R_KVSIB), rs(R_KVSIB), zl, sib)
    kv_sib.start()
    wait_for(left_sib, rs(R_AGSIB))
    wait_for(main_sib, rs(R_KVSIB))

    def attend(q, keys, values, tile):
        q = q.reshape(256, 128)
        scores = [
            lax.dot_general(q, k.reshape(1024, 128), (((1,), (1,)), ((), ())), preferred_element_type=F32)
            * SCORE_SCALE
            for k in keys
        ]
        top = jnp.maximum(
            jnp.max(scores[0], axis=1, keepdims=True), jnp.max(scores[1], axis=1, keepdims=True)
        )
        total = 0.0
        mixed = 0.0
        for half in range(2):
            weights = jnp.exp2(scores[half] - top)
            total = total + jnp.sum(weights, axis=1, keepdims=True)
            mixed = mixed + jnp.dot(
                weights.astype(BF16), values[half].reshape(1024, 128), preferred_element_type=F32
            )
        o_t[:, pl.ds(pl.multiple_of(tile * 256, 256), 256)] = jnp.transpose(mixed / total).astype(BF16)

    def attend_main(tile):
        attend(main[0, pl.ds(tile * 16, 16)], (main[1], main_sib[0]), (main[2], main_sib[1]), tile)

    unit0 = 12 * (x % 2) * (zh // 2) + 4 * (x % 2) * (1 - zh // 2) + 8 * (1 - x % 2) * (zh // 2)
    pair_all = 2 * zl + zh % 2

    def m1_copy(i):
        u = i % 8
        core2 = i // 8
        place = unit0 + u
        z2 = place // 5
        row = pl.multiple_of((place % 5) * 16, 16)
        src = o_t.at[pl.ds(pl.multiple_of(u * 16, 16), 16), pl.ds(pl.multiple_of(core2 * 512, 512), 512)]
        dst = m1.at[pair_all, pl.ds(row, 16)]
        return src, dst, z2, core2

    def m1_left_copy(i):
        odd = i % 2
        core2 = i // 2
        src = o_t.at[
            pl.ds(pl.multiple_of(odd * 64, 16), 64), pl.ds(pl.multiple_of(1024 + core2 * 128, 128), 128)
        ]
        dst = m1.at[
            pair_all, pl.ds(pl.multiple_of(16 * (1 - odd), 16), 64), pl.ds(pl.multiple_of(x * 128, 128), 128)
        ]
        return src, dst, 2 * (zh // 2) + odd, 3 * (1 - odd), core2

    def m1_start(i):
        src, dst, z2, core2 = m1_copy(i)
        mine = jnp.logical_and(jnp.logical_and(z2 == zh, c == zl), core2 == c)

        @pl.when(mine)
        def _():
            pltpu.make_async_copy(src, dst, rs(R_M1)).start()

        @pl.when(jnp.logical_not(mine))
        def _():
            send(src, dst, ss(R_M1), rs(R_M1), c, seq_of(y, x, z2, core2)).start()

    def m1_wait_send(i):
        src, dst, z2, core2 = m1_copy(i)
        mine = jnp.logical_and(jnp.logical_and(z2 == zh, c == zl), core2 == c)

        @pl.when(jnp.logical_not(mine))
        def _():
            send(src, dst, ss(R_M1), rs(R_M1), c, seq_of(y, x, z2, core2)).wait_send()

    def left_mine(x2, z2, core2):
        here = jnp.logical_and(x2 == x, z2 == zh)
        return jnp.logical_and(here, jnp.logical_and(c == zl, core2 == c))

    def m1_left_start(i):
        src, dst, x2, z2, core2 = m1_left_copy(i)
        mine = left_mine(x2, z2, core2)

        @pl.when(mine)
        def _():
            pltpu.make_async_copy(src, dst, rs(R_M1)).start()

        @pl.when(jnp.logical_not(mine))
        def _():
            send(src, dst, ss(R_M1), rs(R_M1), c, seq_of(y, x2, z2, core2)).start()

    def m1_left_wait_send(i):
        src, dst, x2, z2, core2 = m1_left_copy(i)

        @pl.when(jnp.logical_not(left_mine(x2, z2, core2)))
        def _():
            send(src, dst, ss(R_M1), rs(R_M1), c, seq_of(y, x2, z2, core2)).wait_send()

    pl.semaphore_wait(token, 1)

    @pl.loop(0, 2)
    def _(core2):
        @pl.loop(0, 2)
        def _(j):
            attend_main(core2 * 2 + j)

        @pl.loop(0, 8)
        def _(u):
            m1_start(core2 * 8 + u)

    attend(left_q[...], (left[0], left_sib[0]), (left[1], left_sib[1]), 4)

    @pl.loop(0, 4)
    def _(i):
        m1_left_start(i)

    wait_for(w_buf.at[0, pl.ds(0, 12)], rs(R_W))
    w_fwd = send(w_buf.at[c], w_buf.at[c], ss(R_WSIB), rs(R_WSIB), zl, sib)
    w_fwd.start()

    wait_for(m1, rs(R_M1))
    guide = [weight_eighths[i].astype(F32) * GUIDE_UNIT for i in range(4)]
    total = m1[0].astype(F32) * guide[0]
    for i in range(1, 4):
        total = total + m1[i].astype(F32) * guide[i]
    mx[...] = total.astype(BF16)

    def m2_copy(i):
        src = mx.at[:, pl.ds(pl.multiple_of((i // 4) * 128, 128), 128)]
        return src, m2.at[col]

    @pl.loop(1, 16)
    def _(j):
        i = (col + j) % 16
        src, dst = m2_copy(i)
        send(src, dst, ss(R_M2), rs(R_M2), zl, seq_of(i // 4, i % 4, zh, c)).start()

    src, dst = m2_copy(col)
    pltpu.make_async_copy(src, dst, rs(R_M2)).start()

    ranks = jnp.concatenate(
        [
            lax.dot_general(
                down_all[adapter[i]], m1[i], (((0,), (0,)), ((), ())), preferred_element_type=F32
            )
            * guide[i]
            for i in range(4)
        ],
        axis=0,
    )
    lr[...] = jnp.transpose(ranks).astype(BF16)

    def lr_copy(i):
        src = lr.at[pl.ds(pl.multiple_of(i * 32, 32), 32)]
        return src, lr_got.at[col]

    @pl.loop(1, 16)
    def _(j):
        i = (col + j) % 16
        src, dst = lr_copy(i)
        send(src, dst, ss(R_LR), rs(R_LR), zl, seq_of(i // 4, i % 4, zh, c)).start()

    src, dst = lr_copy(col)
    pltpu.make_async_copy(src, dst, rs(R_LR)).start()

    wait_for(w_buf.at[0], rs(R_WSIB))
    wait_for(m2, rs(R_M2))
    rows = jnp.transpose(m2[...].reshape(1280, 128).astype(F32)).astype(BF16)
    for half in range(2):
        p_out[:, 640 * half : 640 * (half + 1)] = jnp.dot(
            rows, w_buf[half].reshape(1280, 640), preferred_element_type=F32
        ).astype(BF16)

    def p_copy(i):
        x2 = 2 * c + i // 4
        z2 = i % 4
        src = p_out.at[pl.ds(pl.multiple_of(i * 16, 16), 16)]
        dst = p_got.at[zh, :, pl.ds(pl.multiple_of((x % 2) * 1280, 1280), 1280)]
        here = jnp.logical_and(jnp.logical_and(x2 == x, z2 == zh), x // 2 == zl)
        return src, dst, seq_of(y, x2, z2, zl), jnp.logical_and(here, c == zl)

    @pl.loop(0, 8)
    def _(i):
        src, dst, to, mine = p_copy(i)

        @pl.when(mine)
        def _():
            pltpu.make_async_copy(src, dst, rs(R_P)).start()

        @pl.when(jnp.logical_not(mine))
        def _():
            send(src, dst, ss(R_P), rs(R_P), x // 2, to).start()

    wait_for(lr_got, rs(R_LR))
    low = lr_got[0].astype(F32)
    for i in range(1, 16):
        low = low + lr_got[i].astype(F32)
    lr_sum[...] = low.astype(BF16)

    def lrf_copy(i):
        x2 = 2 * c + x // 2
        z2 = 2 * (x % 2) + i // 2
        zl2 = i % 2
        src = lr_sum.at[pl.ds(pl.multiple_of((i // 2) * 16, 16), 16)]
        dst = lr_fin.at[zh]
        here = jnp.logical_and(jnp.logical_and(x2 == x, z2 == zh), zl2 == zl)
        return src, dst, zl2, seq_of(y, x2, z2, zl), jnp.logical_and(here, c == zl)

    @pl.loop(0, 4)
    def _(i):
        src, dst, zl2, to, mine = lrf_copy(i)

        @pl.when(mine)
        def _():
            pltpu.make_async_copy(src, dst, rs(R_LRF)).start()

        @pl.when(jnp.logical_not(mine))
        def _():
            send(src, dst, ss(R_LRF), rs(R_LRF), zl2, to).start()

    wait_for(lr_fin, rs(R_LRF))
    low = lr_fin[0].astype(F32)
    for i in range(1, 4):
        low = low + lr_fin[i].astype(F32)
    adapted = jnp.dot(low.astype(BF16), up_cat[...], preferred_element_type=F32)
    wait_for(p_got, rs(R_P))
    for i in range(4):
        adapted = adapted + p_got[i].astype(F32)
    out[...] = adapted

    for copy in sib_copies:
        copy.wait_send()
    wait_for(left.at[:, pl.ds(0, 15)], ss(R_LEFT))
    wait_for(left_q.at[pl.ds(0, 15)], ss(R_LEFTQ))

    @pl.when(x != y)
    def _():
        left_q_far.wait_send()

    wait_for(main.at[:, pl.ds(0, 63)], ss(R_MAIN))
    wait_for(w_buf.at[0, pl.ds(0, 3)], ss(R_WX))
    wait_for(w_buf.at[0, pl.ds(0, 12)], ss(R_W))
    wait_for(left.at[:, pl.ds(0, 48)], ss(R_AG))
    ag_sib.wait_send()
    kv_sib.wait_send()
    w_fwd.wait_send()

    @pl.loop(0, 16)
    def _(i):
        m1_wait_send(i)

    @pl.loop(0, 4)
    def _(i):
        m1_left_wait_send(i)

    wait_for(m2.at[pl.ds(0, 15)], ss(R_M2))
    wait_for(lr_got.at[pl.ds(0, 15)], ss(R_LR))

    @pl.loop(0, 8)
    def _(i):
        src, dst, to, mine = p_copy(i)

        @pl.when(jnp.logical_not(mine))
        def _():
            send(src, dst, ss(R_P), rs(R_P), x // 2, to).wait_send()

    @pl.loop(0, 4)
    def _(i):
        src, dst, zl2, to, mine = lrf_copy(i)

        @pl.when(jnp.logical_not(mine))
        def _():
            send(src, dst, ss(R_LRF), rs(R_LRF), zl2, to).wait_send()


def shards(q, k, v, w, down, up, adapter, weight_eighths, gate_offset, timestep):
    whole = pl.BlockSpec(memory_space=pl.ANY)
    smem = pl.BlockSpec(memory_space=pltpu.SMEM)
    vm = pltpu.VMEM
    mixture = pl.pallas_call(
        body,
        out_shape=jax.ShapeDtypeStruct((16, 2560), F32),
        in_specs=[smem, smem] + [whole] * 6,
        out_specs=pl.BlockSpec(memory_space=pltpu.VMEM),
        scratch_shapes=[
            vm((3, 2, 16, 5120), BF16),
            vm((40, 5120), BF16),
            vm((4, 40, 640), BF16),
            vm((4, 80, 640), BF16),
            vm((2, 16, 80, 640), BF16),
            vm((4, 40, 64), BF16),
            vm((4, 40, 64), BF16),
            vm((4, 80, 64), BF16),
            vm((4, 64, 2560), BF16),
            vm((256, 2560), BF16),
            vm((3, 64, 16, 128), BF16),
            vm((2, 64, 16, 128), BF16),
            vm((16, 16, 128), BF16),
            vm((2, 64, 16, 128), BF16),
            vm((2, 64, 16, 128), BF16),
            vm((128, 1280), BF16),
            vm((4, 80, 512), BF16),
            vm((80, 512), BF16),
            vm((16, 80, 128), BF16),
            vm((512, 256), BF16),
            vm((16, 32, 256), BF16),
            vm((32, 256), BF16),
            vm((128, 1280), BF16),
            vm((4, 16, 2560), BF16),
            vm((4, 16, 256), BF16),
            pltpu.SemaphoreType.DMA((6,)),
            pltpu.SemaphoreType.DMA((16,)),
            pltpu.SemaphoreType.DMA((16,)),
            pltpu.SemaphoreType.REGULAR,
        ],
        compiler_params=pltpu.CompilerParams(
            collective_id=0, has_side_effects=True, vmem_limit_bytes=62 * 2**20
        ),
        name="guided_attention",
    )(adapter, weight_eighths, q, k, v, w, down, up)

    columns = lax.axis_index("branch") * 2560 + jnp.arange(2560, dtype=jnp.int32)
    frequency = jnp.exp((columns % 2560).astype(F32) * (-math.log(10000.0) / 2560))
    angles = timestep.astype(F32)[0] * frequency
    gate_row = gate_offset + jnp.where(columns < 2560, jnp.cos(angles), jnp.sin(angles))
    return (mixture * gate_row[None, :]).astype(BF16)


def solution(mesh):
    placed = (
        P("branch", "seq", None),
        P("branch", "seq", None),
        P("branch", "seq", None),
        P("seq", None),
        P(None, "seq", None),
        P(),
        P(),
        P(),
        P("branch"),
        P(),
    )
    return jax.shard_map(
        shards, mesh=mesh, in_specs=placed, out_specs=P("seq", "branch"), check_vma=False
    )
```

```python
import math

import jax
import jax.numpy as jnp
from jax import lax
from jax.experimental import pallas as pl
from jax.experimental.pallas import tpu as pltpu
from jax.sharding import PartitionSpec as P

MESH = pl.DeviceIdType.MESH
BF16 = jnp.bfloat16
F32 = jnp.float32
HEAD_DIM = 128
GUIDE_UNIT = 0.125
SCORE_SCALE = HEAD_DIM**-0.5 * math.log2(math.e)


def seq_of(y, x, zh, c):
    return ((y * 4 + x) * 4 + zh) * 2 + c


def wait_for(ref, sem):
    pltpu.make_async_copy(ref, ref, sem).wait()


def send(src, dst, send_sem, recv_sem, zl, s):
    return pltpu.make_async_remote_copy(
        src_ref=src, dst_ref=dst, send_sem=send_sem, recv_sem=recv_sem, device_id=(zl, s), device_id_type=MESH
    )


def body(
    adapter,
    weight_eighths,
    q_in,
    k_in,
    v_in,
    w_in,
    down_in,
    up_in,
    out,
    qkv_st,
    w_v,
    w_sib,
    w_st,
    w_buf,
    down_v,
    down_sib,
    down_all,
    up_v,
    up_cat,
    main,
    main_sib,
    left_q,
    left,
    left_sib,
    o_t,
    m1,
    mx,
    m2,
    lr,
    lr_got,
    lr_sum,
    p_out,
    p_got,
    lr_fin,
    in_sem,
    send_sem,
    recv_sem,
    token,
):
    s = lax.axis_index("seq")
    zl = lax.axis_index("branch")
    c = s % 2
    chip = s // 2
    zh = chip % 4
    x = (chip // 4) % 4
    y = chip // 16
    col = chip // 4
    sib = s + 1 - 2 * c
    slot_left = (x // 2) * 8 + (x % 2) * 4 + zh
    slot = (x // 2) * 32 + y * 8 + (x % 2) * 4 + zh
    (
        R_SIBW,
        R_LEFT,
        R_LEFTQ,
        R_MAIN,
        R_Q,
        R_AG,
        R_AGSIB,
        R_KVSIB,
        R_W,
        R_WSIB,
        R_M1,
        R_M2,
        R_LR,
        R_P,
        R_LRF,
        R_SIBD,
        R_WX,
        R_QS,
    ) = range(18)

    def rs(i):
        return recv_sem.at[i]

    def ss(i):
        return send_sem.at[i]

    loads = [
        pltpu.make_async_copy(w_in, w_v, in_sem.at[0]),
        pltpu.make_async_copy(down_in, down_v, in_sem.at[1]),
        pltpu.make_async_copy(k_in, qkv_st.at[1], in_sem.at[2]),
        pltpu.make_async_copy(v_in, qkv_st.at[2], in_sem.at[3]),
        pltpu.make_async_copy(q_in, qkv_st.at[0], in_sem.at[4]),
        pltpu.make_async_copy(up_in.at[:, :, pl.ds(pl.multiple_of(zl * 2560, 2560), 2560)], up_v, in_sem.at[5]),
    ]
    for load in loads:
        load.start()

    barrier = pltpu.get_barrier_semaphore()

    @pl.loop(1, 64)
    def _(i):
        pl.semaphore_signal(barrier, 1, device_id=(zl, ((chip + i) % 64) * 2 + c), device_id_type=MESH)

    pl.semaphore_signal(barrier, 1, device_id=(zl, sib), device_id_type=MESH)
    pl.semaphore_signal(barrier, 1, device_id=(1 - zl, s), device_id_type=MESH)
    for load in loads[:5]:
        load.wait()
    pl.semaphore_wait(barrier, 65)

    sib_copies = [
        send(
            w_v.at[:, pl.ds(pl.multiple_of(1280 * i + 640 * (1 - c), 128), 640)],
            w_sib.at[i],
            ss(R_SIBW),
            rs(R_SIBW),
            zl,
            sib,
        )
        for i in range(4)
    ]
    sib_copies.append(send(down_v, down_sib, ss(R_SIBD), rs(R_SIBD), zl, sib))
    for copy in sib_copies:
        copy.start()

    wait_for(w_sib, rs(R_SIBW))
    wait_for(down_sib, rs(R_SIBD))
    pl.semaphore_signal(token, 1, device_id=(1 - zl, s), device_id_type=MESH)

    def joined(own, other):
        first = jnp.where(c == 0, own, other)
        second = jnp.where(c == 0, other, own)
        return jnp.concatenate([first, second], axis=0).astype(BF16)

    for i in range(4):
        own = w_v[:, pl.ds(pl.multiple_of(1280 * i + 640 * c, 128), 640)].astype(F32)
        w_st[i] = joined(own, w_sib[i].astype(F32))
    for j in range(1, 4):
        i = (x + j) % 4
        send(w_st.at[i], w_buf.at[c, col], ss(R_WX), rs(R_WX), zl, seq_of(y, i, zh, c)).start()
    pltpu.make_async_copy(w_st.at[x], w_buf.at[c, col], rs(R_WX)).start()

    def left_copy(i):
        y2 = i // 4
        z2 = i % 4
        head = 5 * (2 * y2 + z2 // 2) + 2
        lanes = pl.ds(pl.multiple_of(head * 128, 128), 128)
        pair = z2 % 2
        return (
            (qkv_st.at[pl.ds(1, 2), pair, :, lanes], left.at[:, x * 16 + y * 4 + zh], R_LEFT),
            (qkv_st.at[0, pair, :, lanes], left_q.at[slot_left], R_LEFTQ),
        )

    @pl.loop(1, 16)
    def _(j):
        i = (y * 4 + zh + j) % 16
        (src, dst, n), (src_q, dst_q, n_q) = left_copy(i)
        send(src, dst, ss(n), rs(n), zl, seq_of(i // 4, x, i % 4, c)).start()
        send(src_q, dst_q, ss(n_q), rs(n_q), zl, seq_of(i // 4, y, i % 4, c)).start()

    (src, dst, n), (src_q, dst_q, n_q) = left_copy(y * 4 + zh)
    pltpu.make_async_copy(src, dst, rs(n)).start()
    left_q_far = send(src_q, dst_q, ss(n_q), rs(n_q), zl, seq_of(y, y, zh, c))

    @pl.when(x == y)
    def _():
        pltpu.make_async_copy(src_q, dst_q, rs(n_q)).start()

    @pl.when(x != y)
    def _():
        left_q_far.start()

    def main_copy(i):
        y2 = i // 16
        x2 = (i // 4) % 4
        z2 = i % 4
        head = 5 * (2 * y2 + x2 // 2) + 3 * (x2 % 2) + z2 // 2
        lanes = pl.ds(pl.multiple_of(head * 128, 128), 128)
        pair = z2 % 2
        return (
            (qkv_st.at[pl.ds(1, 2), pair, :, lanes], main.at[pl.ds(1, 2), slot]),
            (qkv_st.at[0, pair, :, lanes], main.at[0, slot]),
        )

    def kv_start(j):
        i = (chip + j) % 64
        src, dst = main_copy(i)[0]
        send(src, dst, ss(R_MAIN), rs(R_MAIN), zl, i * 2 + c).start()

    @pl.loop(1, 24)
    def _(j):
        kv_start(j)

    slab = left.at[:, pl.ds(x * 16, 16)]
    wait_for(slab, rs(R_LEFT))
    for j in range(1, 4):
        send(slab, slab, ss(R_AG), rs(R_AG), zl, seq_of(y, (x + j) % 4, zh, c)).start()

    @pl.loop(24, 64)
    def _(j):
        kv_start(j)

    src, dst = main_copy(chip)[0]
    pltpu.make_async_copy(src, dst, rs(R_MAIN)).start()

    def flip(a, bit):
        return (a + bit) % 2

    def query_start(i):
        x2 = 2 * flip(x // 2, i // 32) + flip(x % 2, (i // 4) % 2)
        y2 = 2 * flip(y // 2, (i // 16) % 2) + flip(y % 2, (i // 8) % 2)
        to = (y2 * 4 + x2) * 4 + (zh + i) % 4
        src, dst = main_copy(to)[1]
        send(src, dst, ss(R_Q), rs(R_QS + i // 16), zl, to * 2 + c).start()

    src, dst = main_copy(chip)[1]
    pltpu.make_async_copy(src, dst, rs(R_QS)).start()

    w_slab = w_buf.at[c, pl.ds(y * 4, 4)]
    wait_for(w_slab, rs(R_WX))
    w_own_fwd = send(w_slab, w_slab, ss(R_WSIB), rs(R_WSIB), zl, sib)
    w_own_fwd.start()

    @pl.loop(1, 64)
    def _(i):
        query_start(i)

    for j in range(1, 4):
        send(w_slab, w_slab, ss(R_W), rs(R_W), zl, seq_of((y + j) % 4, x, zh, c)).start()

    for i in range(4):
        down_all[i] = joined(down_v[i].astype(F32), down_sib[i].astype(F32))
    loads[5].wait()
    for i in range(4):
        up_cat[64 * i : 64 * (i + 1), :] = up_v[adapter[i]]

    wait_for(left_q, rs(R_LEFTQ))
    wait_for(left.at[:, pl.ds(0, 48)], rs(R_AG))
    ag_sib = send(left, left_sib, ss(R_AGSIB), rs(R_AGSIB), zl, sib)
    ag_sib.start()
    main_kv = main.at[pl.ds(1, 2)]
    wait_for(main_kv, rs(R_MAIN))
    kv_sib = send(main_kv, main_sib, ss(R_KVSIB), rs(R_KVSIB), zl, sib)
    kv_sib.start()
    wait_for(left_sib, rs(R_AGSIB))

    def attend(q, keys, values, tile):
        q = q.reshape(256, 128)
        scores = [
            lax.dot_general(q, k.reshape(1024, 128), (((1,), (1,)), ((), ())), preferred_element_type=F32)
            * SCORE_SCALE
            for k in keys
        ]
        top = jnp.maximum(
            jnp.max(scores[0], axis=1, keepdims=True), jnp.max(scores[1], axis=1, keepdims=True)
        )
        total = 0.0
        mixed = 0.0
        for half in range(2):
            weights = jnp.exp2(scores[half] - top)
            total = total + jnp.sum(weights, axis=1, keepdims=True)
            mixed = mixed + jnp.dot(
                weights.astype(BF16), values[half].reshape(1024, 128), preferred_element_type=F32
            )
        o_t[:, pl.ds(pl.multiple_of(tile * 256, 256), 256)] = jnp.transpose(mixed / total).astype(BF16)

    def attend_main(tile):
        attend(main[0, pl.ds(tile * 16, 16)], (main[1], main_sib[0]), (main[2], main_sib[1]), tile)

    places = (
        ((0, 0), ((0, 80, 0, 0), (80, 48, 1, 0))),
        ((0, 1), ((0, 32, 1, 48), (32, 80, 2, 0), (112, 16, 3, 0))),
        ((1, 0), ((0, 16, 0, 64), (16, 80, 1, 0), (96, 32, 2, 0))),
        ((1, 1), ((0, 48, 2, 32), (48, 80, 3, 0))),
    )
    pair_all = 2 * zl + zh % 2

    def m1_each(tile, action):
        core2 = tile // 2
        lanes = pl.ds(pl.multiple_of((tile % 2) * 256, 256), 256)
        for (odd, which), pieces in places:

            @pl.when(jnp.logical_and(x % 2 == odd, zh // 2 == which))
            def _():
                for first, count, z2, row in pieces:
                    src = o_t.at[pl.ds(first, count), pl.ds(pl.multiple_of(tile * 256, 256), 256)]
                    dst = m1.at[pair_all, pl.ds(row, count), lanes]
                    mine = jnp.logical_and(jnp.logical_and(z2 == zh, c == zl), core2 == c)
                    action(src, dst, mine, seq_of(y, x, z2, core2))

    def m1_start(src, dst, mine, to):
        @pl.when(mine)
        def _():
            pltpu.make_async_copy(src, dst, rs(R_M1)).start()

        @pl.when(jnp.logical_not(mine))
        def _():
            send(src, dst, ss(R_M1), rs(R_M1), c, to).start()

    def m1_wait_send(src, dst, mine, to):
        @pl.when(jnp.logical_not(mine))
        def _():
            send(src, dst, ss(R_M1), rs(R_M1), c, to).wait_send()

    def m1_left_copy(i):
        odd = i % 2
        core2 = i // 2
        src = o_t.at[
            pl.ds(pl.multiple_of(odd * 64, 16), 64), pl.ds(pl.multiple_of(1024 + core2 * 128, 128), 128)
        ]
        dst = m1.at[
            pair_all, pl.ds(pl.multiple_of(16 * (1 - odd), 16), 64), pl.ds(pl.multiple_of(x * 128, 128), 128)
        ]
        return src, dst, 2 * (zh // 2) + odd, 3 * (1 - odd), core2

    def left_mine(x2, z2, core2):
        here = jnp.logical_and(x2 == x, z2 == zh)
        return jnp.logical_and(here, jnp.logical_and(c == zl, core2 == c))

    def m1_left_start(i):
        src, dst, x2, z2, core2 = m1_left_copy(i)
        mine = left_mine(x2, z2, core2)

        @pl.when(mine)
        def _():
            pltpu.make_async_copy(src, dst, rs(R_M1)).start()

        @pl.when(jnp.logical_not(mine))
        def _():
            send(src, dst, ss(R_M1), rs(R_M1), c, seq_of(y, x2, z2, core2)).start()

    def m1_left_wait_send(i):
        src, dst, x2, z2, core2 = m1_left_copy(i)

        @pl.when(jnp.logical_not(left_mine(x2, z2, core2)))
        def _():
            send(src, dst, ss(R_M1), rs(R_M1), c, seq_of(y, x2, z2, core2)).wait_send()

    pl.semaphore_wait(token, 1)
    attend(left_q[...], (left[0], left_sib[0]), (left[1], left_sib[1]), 4)

    @pl.loop(0, 4)
    def _(i):
        m1_left_start(i)

    wait_for(main_sib, rs(R_KVSIB))

    @pl.loop(0, 4)
    def _(t):
        tile = 2 * flip(x // 2, t // 2) + flip(y // 2, t % 2)
        wait_for(main.at[0, pl.ds(0, 16)], rs(R_QS + t))
        attend_main(tile)

        m1_each(tile, m1_start)

    wait_for(m1, rs(R_M1))
    guide = [weight_eighths[i].astype(F32) * GUIDE_UNIT for i in range(4)]
    total = m1[0].astype(F32) * guide[0]
    for i in range(1, 4):
        total = total + m1[i].astype(F32) * guide[i]
    mx[...] = total.astype(BF16)

    def m2_copy(i):
        src = mx.at[:, pl.ds(pl.multiple_of((i // 4) * 128, 128), 128)]
        return src, m2.at[col]

    @pl.loop(1, 16)
    def _(j):
        i = (col + j) % 16
        src, dst = m2_copy(i)
        send(src, dst, ss(R_M2), rs(R_M2), zl, seq_of(i // 4, i % 4, zh, c)).start()

    src, dst = m2_copy(col)
    pltpu.make_async_copy(src, dst, rs(R_M2)).start()

    wait_for(w_buf.at[0, pl.ds(0, 12)], rs(R_W))

    def w_fwd(j):
        rows = w_buf.at[c, pl.ds((y + j) % 4 * 4, 4)]
        return send(rows, rows, ss(R_WSIB), rs(R_WSIB), zl, sib)

    for j in range(1, 4):
        w_fwd(j).start()

    ranks = jnp.concatenate(
        [
            lax.dot_general(
                down_all[adapter[i]], m1[i], (((0,), (0,)), ((), ())), preferred_element_type=F32
            )
            * guide[i]
            for i in range(4)
        ],
        axis=0,
    )
    lr[...] = jnp.transpose(ranks).astype(BF16)

    def lr_copy(i):
        src = lr.at[pl.ds(pl.multiple_of(i * 32, 32), 32)]
        return src, lr_got.at[col]

    @pl.loop(1, 16)
    def _(j):
        i = (col + j) % 16
        src, dst = lr_copy(i)
        send(src, dst, ss(R_LR), rs(R_LR), zl, seq_of(i // 4, i % 4, zh, c)).start()

    src, dst = lr_copy(col)
    pltpu.make_async_copy(src, dst, rs(R_LR)).start()

    wait_for(w_buf.at[0], rs(R_WSIB))
    wait_for(m2, rs(R_M2))
    rows = jnp.transpose(m2[...].reshape(1280, 128).astype(F32)).astype(BF16)
    def project(half):
        p_out[:, 640 * half : 640 * (half + 1)] = jnp.dot(
            rows, w_buf[half].reshape(1280, 640), preferred_element_type=F32
        ).astype(BF16)

    def p_copy(i, half):
        x2 = 2 * c + i // 4
        z2 = i % 4
        src = p_out.at[pl.ds(pl.multiple_of(i * 16, 16), 16), pl.ds(640 * half, 640)]
        dst = p_got.at[zh, :, pl.ds(pl.multiple_of((x % 2) * 1280 + 640 * half, 128), 640)]
        here = jnp.logical_and(jnp.logical_and(x2 == x, z2 == zh), x // 2 == zl)
        return src, dst, seq_of(y, x2, z2, zl), jnp.logical_and(here, c == zl)

    def p_start(half):
        @pl.loop(0, 8)
        def _(i):
            src, dst, to, mine = p_copy(i, half)

            @pl.when(mine)
            def _():
                pltpu.make_async_copy(src, dst, rs(R_P)).start()

            @pl.when(jnp.logical_not(mine))
            def _():
                send(src, dst, ss(R_P), rs(R_P), x // 2, to).start()

    project(0)
    p_start(0)
    project(1)
    p_start(1)

    wait_for(lr_got, rs(R_LR))
    low = lr_got[0].astype(F32)
    for i in range(1, 16):
        low = low + lr_got[i].astype(F32)
    lr_sum[...] = low.astype(BF16)

    def lrf_copy(i):
        x2 = 2 * c + x // 2
        z2 = 2 * (x % 2) + i // 2
        zl2 = i % 2
        src = lr_sum.at[pl.ds(pl.multiple_of((i // 2) * 16, 16), 16)]
        dst = lr_fin.at[zh]
        here = jnp.logical_and(jnp.logical_and(x2 == x, z2 == zh), zl2 == zl)
        return src, dst, zl2, seq_of(y, x2, z2, zl), jnp.logical_and(here, c == zl)

    @pl.loop(0, 4)
    def _(i):
        src, dst, zl2, to, mine = lrf_copy(i)

        @pl.when(mine)
        def _():
            pltpu.make_async_copy(src, dst, rs(R_LRF)).start()

        @pl.when(jnp.logical_not(mine))
        def _():
            send(src, dst, ss(R_LRF), rs(R_LRF), zl2, to).start()

    wait_for(lr_fin, rs(R_LRF))
    low = lr_fin[0].astype(F32)
    for i in range(1, 4):
        low = low + lr_fin[i].astype(F32)
    adapted = jnp.dot(low.astype(BF16), up_cat[...], preferred_element_type=F32)
    wait_for(p_got, rs(R_P))
    for i in range(4):
        adapted = adapted + p_got[i].astype(F32)
    out[...] = adapted

    for copy in sib_copies:
        copy.wait_send()
    wait_for(left.at[:, pl.ds(0, 15)], ss(R_LEFT))
    wait_for(left_q.at[pl.ds(0, 15)], ss(R_LEFTQ))

    @pl.when(x != y)
    def _():
        left_q_far.wait_send()

    wait_for(main.at[pl.ds(1, 2), pl.ds(0, 63)], ss(R_MAIN))
    wait_for(main.at[0, pl.ds(0, 63)], ss(R_Q))
    wait_for(w_buf.at[0, pl.ds(0, 3)], ss(R_WX))
    wait_for(w_buf.at[0, pl.ds(0, 12)], ss(R_W))
    wait_for(left.at[:, pl.ds(0, 48)], ss(R_AG))
    ag_sib.wait_send()
    kv_sib.wait_send()
    wait_for(w_buf.at[0], ss(R_WSIB))

    @pl.loop(0, 4)
    def _(tile):
        m1_each(tile, m1_wait_send)

    @pl.loop(0, 4)
    def _(i):
        m1_left_wait_send(i)

    wait_for(m2.at[pl.ds(0, 15)], ss(R_M2))
    wait_for(lr_got.at[pl.ds(0, 15)], ss(R_LR))

    for half in range(2):

        @pl.loop(0, 8)
        def _(i):
            src, dst, to, mine = p_copy(i, half)

            @pl.when(jnp.logical_not(mine))
            def _():
                send(src, dst, ss(R_P), rs(R_P), x // 2, to).wait_send()

    @pl.loop(0, 4)
    def _(i):
        src, dst, zl2, to, mine = lrf_copy(i)

        @pl.when(jnp.logical_not(mine))
        def _():
            send(src, dst, ss(R_LRF), rs(R_LRF), zl2, to).wait_send()


def shards(q, k, v, w, down, up, adapter, weight_eighths, gate_offset, timestep):
    whole = pl.BlockSpec(memory_space=pl.ANY)
    smem = pl.BlockSpec(memory_space=pltpu.SMEM)
    vm = pltpu.VMEM
    mixture = pl.pallas_call(
        body,
        out_shape=jax.ShapeDtypeStruct((16, 2560), F32),
        in_specs=[smem, smem] + [whole] * 6,
        out_specs=pl.BlockSpec(memory_space=pltpu.VMEM),
        scratch_shapes=[
            vm((3, 2, 16, 5120), BF16),
            vm((40, 5120), BF16),
            vm((4, 40, 640), BF16),
            vm((4, 80, 640), BF16),
            vm((2, 16, 80, 640), BF16),
            vm((4, 40, 64), BF16),
            vm((4, 40, 64), BF16),
            vm((4, 80, 64), BF16),
            vm((4, 64, 2560), BF16),
            vm((256, 2560), BF16),
            vm((3, 64, 16, 128), BF16),
            vm((2, 64, 16, 128), BF16),
            vm((16, 16, 128), BF16),
            vm((2, 64, 16, 128), BF16),
            vm((2, 64, 16, 128), BF16),
            vm((128, 1280), BF16),
            vm((4, 80, 512), BF16),
            vm((80, 512), BF16),
            vm((16, 80, 128), BF16),
            vm((512, 256), BF16),
            vm((16, 32, 256), BF16),
            vm((32, 256), BF16),
            vm((128, 1280), BF16),
            vm((4, 16, 2560), BF16),
            vm((4, 16, 256), BF16),
            pltpu.SemaphoreType.DMA((6,)),
            pltpu.SemaphoreType.DMA((17,)),
            pltpu.SemaphoreType.DMA((21,)),
            pltpu.SemaphoreType.REGULAR,
        ],
        compiler_params=pltpu.CompilerParams(
            collective_id=0, has_side_effects=True, vmem_limit_bytes=62 * 2**20
        ),
        name="guided_attention",
    )(adapter, weight_eighths, q, k, v, w, down, up)

    columns = lax.axis_index("branch") * 2560 + jnp.arange(2560, dtype=jnp.int32)
    frequency = jnp.exp((columns % 2560).astype(F32) * (-math.log(10000.0) / 2560))
    angles = timestep.astype(F32)[0] * frequency
    gate_row = gate_offset + jnp.where(columns < 2560, jnp.cos(angles), jnp.sin(angles))
    return (mixture * gate_row[None, :]).astype(BF16)


def solution(mesh):
    placed = (
        P("branch", "seq", None),
        P("branch", "seq", None),
        P("branch", "seq", None),
        P("seq", None),
        P(None, "seq", None),
        P(),
        P(),
        P(),
        P("branch"),
        P(),
    )
    return jax.shard_map(
        shards, mesh=mesh, in_specs=placed, out_specs=P("seq", "branch"), check_vma=False
    )
```

```python
import math

import jax
import jax.numpy as jnp
from jax import lax
from jax.experimental import pallas as pl
from jax.experimental.pallas import tpu as pltpu
from jax.sharding import PartitionSpec as P

MESH = pl.DeviceIdType.MESH
BF16 = jnp.bfloat16
F32 = jnp.float32
HEAD_DIM = 128
GUIDE_UNIT = 0.125
SCORE_SCALE = HEAD_DIM**-0.5 * math.log2(math.e)


def seq_of(y, x, zh, c):
    return ((y * 4 + x) * 4 + zh) * 2 + c


def wait_for(ref, sem):
    pltpu.make_async_copy(ref, ref, sem).wait()


def send(src, dst, send_sem, recv_sem, zl, s):
    return pltpu.make_async_remote_copy(
        src_ref=src, dst_ref=dst, send_sem=send_sem, recv_sem=recv_sem, device_id=(zl, s), device_id_type=MESH
    )


def body(
    adapter,
    weight_eighths,
    q_in,
    k_in,
    v_in,
    w_in,
    down_in,
    up_in,
    out,
    qkv_st,
    w_v,
    w_sib,
    w_st,
    w_buf,
    down_v,
    down_sib,
    down_all,
    up_v,
    up_cat,
    main,
    main_sib,
    left_q,
    left,
    left_sib,
    o_t,
    m1,
    mx,
    m2,
    lr,
    lr_got,
    lr_sum,
    p_out,
    p_got,
    lr_fin,
    in_sem,
    send_sem,
    recv_sem,
    token,
):
    s = lax.axis_index("seq")
    zl = lax.axis_index("branch")
    c = s % 2
    chip = s // 2
    zh = chip % 4
    x = (chip // 4) % 4
    y = chip // 16
    col = chip // 4
    sib = s + 1 - 2 * c
    slot_left = (x // 2) * 8 + (x % 2) * 4 + zh
    slot = (x // 2) * 32 + y * 8 + (x % 2) * 4 + zh
    (
        R_SIBW,
        R_LEFT,
        R_LEFTQ,
        R_MAIN,
        R_Q,
        R_AG,
        R_AGSIB,
        R_KVSIB,
        R_W,
        R_WSIB,
        R_M1,
        R_M2,
        R_LR,
        R_P,
        R_LRF,
        R_SIBD,
        R_WX,
        R_QS,
    ) = range(18)

    def rs(i):
        return recv_sem.at[i]

    def ss(i):
        return send_sem.at[i]

    loads = [
        pltpu.make_async_copy(w_in, w_v, in_sem.at[0]),
        pltpu.make_async_copy(down_in, down_v, in_sem.at[1]),
        pltpu.make_async_copy(k_in, qkv_st.at[1], in_sem.at[2]),
        pltpu.make_async_copy(v_in, qkv_st.at[2], in_sem.at[3]),
        pltpu.make_async_copy(q_in, qkv_st.at[0], in_sem.at[4]),
        pltpu.make_async_copy(up_in.at[:, :, pl.ds(pl.multiple_of(zl * 2560, 2560), 2560)], up_v, in_sem.at[5]),
    ]
    for load in loads:
        load.start()

    barrier = pltpu.get_barrier_semaphore()

    @pl.loop(1, 64)
    def _(i):
        pl.semaphore_signal(barrier, 1, device_id=(zl, ((chip + i) % 64) * 2 + c), device_id_type=MESH)

    pl.semaphore_signal(barrier, 1, device_id=(zl, sib), device_id_type=MESH)
    pl.semaphore_signal(barrier, 1, device_id=(1 - zl, s), device_id_type=MESH)
    for load in loads[:5]:
        load.wait()
    pl.semaphore_wait(barrier, 65)

    sib_copies = [
        send(
            w_v.at[:, pl.ds(pl.multiple_of(640 * i + 2560 * (1 - c), 128), 640)],
            w_sib.at[i],
            ss(R_SIBW),
            rs(R_SIBW),
            zl,
            sib,
        )
        for i in range(4)
    ]
    sib_copies.append(send(down_v, down_sib, ss(R_SIBD), rs(R_SIBD), zl, sib))
    for copy in sib_copies:
        copy.start()

    wait_for(w_sib, rs(R_SIBW))
    wait_for(down_sib, rs(R_SIBD))
    pl.semaphore_signal(token, 1, device_id=(1 - zl, s), device_id_type=MESH)

    def joined(own, other):
        first = jnp.where(c == 0, own, other)
        second = jnp.where(c == 0, other, own)
        return jnp.concatenate([first, second], axis=0).astype(BF16)

    for i in range(4):
        own = w_v[:, pl.ds(pl.multiple_of(640 * i + 2560 * c, 128), 640)].astype(F32)
        w_st[i] = joined(own, w_sib[i].astype(F32))
    for j in range(1, 4):
        i = (x + j) % 4
        send(w_st.at[i], w_buf.at[c, col], ss(R_WX), rs(R_WX), zl, seq_of(y, i, zh, c)).start()
    pltpu.make_async_copy(w_st.at[x], w_buf.at[c, col], rs(R_WX)).start()

    def left_copy(i):
        y2 = i // 4
        z2 = i % 4
        head = 5 * (2 * y2 + z2 // 2) + 2
        lanes = pl.ds(pl.multiple_of(head * 128, 128), 128)
        pair = z2 % 2
        return (
            (qkv_st.at[pl.ds(1, 2), pair, :, lanes], left.at[:, x * 16 + y * 4 + zh], R_LEFT),
            (qkv_st.at[0, pair, :, lanes], left_q.at[slot_left], R_LEFTQ),
        )

    @pl.loop(1, 16)
    def _(j):
        i = (y * 4 + zh + j) % 16
        (src, dst, n), (src_q, dst_q, n_q) = left_copy(i)
        send(src, dst, ss(n), rs(n), zl, seq_of(i // 4, x, i % 4, c)).start()
        send(src_q, dst_q, ss(n_q), rs(n_q), zl, seq_of(i // 4, y, i % 4, c)).start()

    (src, dst, n), (src_q, dst_q, n_q) = left_copy(y * 4 + zh)
    pltpu.make_async_copy(src, dst, rs(n)).start()
    left_q_far = send(src_q, dst_q, ss(n_q), rs(n_q), zl, seq_of(y, y, zh, c))

    @pl.when(x == y)
    def _():
        pltpu.make_async_copy(src_q, dst_q, rs(n_q)).start()

    @pl.when(x != y)
    def _():
        left_q_far.start()

    def main_copy(i):
        y2 = i // 16
        x2 = (i // 4) % 4
        z2 = i % 4
        head = 5 * (2 * y2 + x2 // 2) + 3 * (x2 % 2) + z2 // 2
        lanes = pl.ds(pl.multiple_of(head * 128, 128), 128)
        pair = z2 % 2
        return (
            (qkv_st.at[pl.ds(1, 2), pair, :, lanes], main.at[pl.ds(1, 2), slot]),
            (qkv_st.at[0, pair, :, lanes], main.at[0, slot]),
        )

    def kv_start(j):
        i = (chip + j) % 64
        src, dst = main_copy(i)[0]
        send(src, dst, ss(R_MAIN), rs(R_MAIN), zl, i * 2 + c).start()

    @pl.loop(1, 24)
    def _(j):
        kv_start(j)

    slab = left.at[:, pl.ds(x * 16, 16)]
    wait_for(slab, rs(R_LEFT))
    for j in range(1, 4):
        send(slab, slab, ss(R_AG), rs(R_AG), zl, seq_of(y, (x + j) % 4, zh, c)).start()

    @pl.loop(24, 64)
    def _(j):
        kv_start(j)

    src, dst = main_copy(chip)[0]
    pltpu.make_async_copy(src, dst, rs(R_MAIN)).start()

    def flip(a, bit):
        return (a + bit) % 2

    def query_start(i):
        x2 = 2 * flip(x // 2, i // 32) + flip(x % 2, (i // 4) % 2)
        y2 = 2 * flip(y // 2, (i // 16) % 2) + flip(y % 2, (i // 8) % 2)
        to = (y2 * 4 + x2) * 4 + (zh + i) % 4
        src, dst = main_copy(to)[1]
        send(src, dst, ss(R_Q), rs(R_QS + i // 16), zl, to * 2 + c).start()

    src, dst = main_copy(chip)[1]
    pltpu.make_async_copy(src, dst, rs(R_QS)).start()

    w_slab = w_buf.at[c, pl.ds(y * 4, 4)]
    wait_for(w_slab, rs(R_WX))
    w_own_fwd = send(w_slab, w_slab, ss(R_WSIB), rs(R_WSIB), zl, sib)
    w_own_fwd.start()

    @pl.loop(1, 64)
    def _(i):
        query_start(i)

    for j in range(1, 4):
        send(w_slab, w_slab, ss(R_W), rs(R_W), zl, seq_of((y + j) % 4, x, zh, c)).start()

    for i in range(4):
        down_all[i] = joined(down_v[i].astype(F32), down_sib[i].astype(F32))
    loads[5].wait()
    for i in range(4):
        up_cat[64 * i : 64 * (i + 1), :] = up_v[adapter[i]]

    wait_for(left_q, rs(R_LEFTQ))
    wait_for(left.at[:, pl.ds(0, 48)], rs(R_AG))
    ag_sib = send(left, left_sib, ss(R_AGSIB), rs(R_AGSIB), zl, sib)
    ag_sib.start()
    main_kv = main.at[pl.ds(1, 2)]
    wait_for(main_kv, rs(R_MAIN))
    kv_sib = send(main_kv, main_sib, ss(R_KVSIB), rs(R_KVSIB), zl, sib)
    kv_sib.start()
    wait_for(left_sib, rs(R_AGSIB))

    def attend(q, keys, values, tile):
        q = q.reshape(256, 128)
        scores = [
            lax.dot_general(q, k.reshape(1024, 128), (((1,), (1,)), ((), ())), preferred_element_type=F32)
            * SCORE_SCALE
            for k in keys
        ]
        top = jnp.maximum(
            jnp.max(scores[0], axis=1, keepdims=True), jnp.max(scores[1], axis=1, keepdims=True)
        )
        total = 0.0
        mixed = 0.0
        for half in range(2):
            weights = jnp.exp2(scores[half] - top)
            total = total + jnp.sum(weights, axis=1, keepdims=True)
            mixed = mixed + jnp.dot(
                weights.astype(BF16), values[half].reshape(1024, 128), preferred_element_type=F32
            )
        o_t[:, pl.ds(pl.multiple_of(tile * 256, 256), 256)] = jnp.transpose(mixed / total).astype(BF16)

    def attend_main(tile):
        attend(main[0, pl.ds(tile * 16, 16)], (main[1], main_sib[0]), (main[2], main_sib[1]), tile)

    places = (
        ((0, 0), ((0, 80, 0, 0), (80, 48, 1, 0))),
        ((0, 1), ((0, 32, 1, 48), (32, 80, 2, 0), (112, 16, 3, 0))),
        ((1, 0), ((0, 16, 0, 64), (16, 80, 1, 0), (96, 32, 2, 0))),
        ((1, 1), ((0, 48, 2, 32), (48, 80, 3, 0))),
    )
    pair_all = 2 * zl + zh % 2

    def m1_each(tile, action):
        core2 = tile // 2
        lanes = pl.ds(pl.multiple_of((tile % 2) * 256, 256), 256)
        for (odd, which), pieces in places:

            @pl.when(jnp.logical_and(x % 2 == odd, zh // 2 == which))
            def _():
                for first, count, z2, row in pieces:
                    src = o_t.at[pl.ds(first, count), pl.ds(pl.multiple_of(tile * 256, 256), 256)]
                    dst = m1.at[pair_all, pl.ds(row, count), lanes]
                    mine = jnp.logical_and(jnp.logical_and(z2 == zh, c == zl), core2 == c)
                    action(src, dst, mine, seq_of(y, x, z2, core2))

    def m1_start(src, dst, mine, to):
        @pl.when(mine)
        def _():
            pltpu.make_async_copy(src, dst, rs(R_M1)).start()

        @pl.when(jnp.logical_not(mine))
        def _():
            send(src, dst, ss(R_M1), rs(R_M1), c, to).start()

    def m1_wait_send(src, dst, mine, to):
        @pl.when(jnp.logical_not(mine))
        def _():
            send(src, dst, ss(R_M1), rs(R_M1), c, to).wait_send()

    def m1_left_copy(i):
        odd = i % 2
        core2 = i // 2
        src = o_t.at[
            pl.ds(pl.multiple_of(odd * 64, 16), 64), pl.ds(pl.multiple_of(1024 + core2 * 128, 128), 128)
        ]
        dst = m1.at[
            pair_all, pl.ds(pl.multiple_of(16 * (1 - odd), 16), 64), pl.ds(pl.multiple_of(x * 128, 128), 128)
        ]
        return src, dst, 2 * (zh // 2) + odd, 3 * (1 - odd), core2

    def left_mine(x2, z2, core2):
        here = jnp.logical_and(x2 == x, z2 == zh)
        return jnp.logical_and(here, jnp.logical_and(c == zl, core2 == c))

    def m1_left_start(i):
        src, dst, x2, z2, core2 = m1_left_copy(i)
        mine = left_mine(x2, z2, core2)

        @pl.when(mine)
        def _():
            pltpu.make_async_copy(src, dst, rs(R_M1)).start()

        @pl.when(jnp.logical_not(mine))
        def _():
            send(src, dst, ss(R_M1), rs(R_M1), c, seq_of(y, x2, z2, core2)).start()

    def m1_left_wait_send(i):
        src, dst, x2, z2, core2 = m1_left_copy(i)

        @pl.when(jnp.logical_not(left_mine(x2, z2, core2)))
        def _():
            send(src, dst, ss(R_M1), rs(R_M1), c, seq_of(y, x2, z2, core2)).wait_send()

    pl.semaphore_wait(token, 1)
    attend(left_q[...], (left[0], left_sib[0]), (left[1], left_sib[1]), 4)

    @pl.loop(0, 4)
    def _(i):
        m1_left_start(i)

    wait_for(main_sib, rs(R_KVSIB))

    @pl.loop(0, 4)
    def _(t):
        tile = 2 * flip(x // 2, t // 2) + flip(y // 2, t % 2)
        wait_for(main.at[0, pl.ds(0, 16)], rs(R_QS + t))
        attend_main(tile)

        m1_each(tile, m1_start)

    wait_for(m1, rs(R_M1))
    guide = [weight_eighths[i].astype(F32) * GUIDE_UNIT for i in range(4)]
    total = m1[0].astype(F32) * guide[0]
    for i in range(1, 4):
        total = total + m1[i].astype(F32) * guide[i]
    mx[...] = total.astype(BF16)

    def m2_copy(i):
        src = mx.at[:, pl.ds(pl.multiple_of((i // 4) * 128, 128), 128)]
        return src, m2.at[col]

    @pl.loop(1, 16)
    def _(j):
        i = (col + j) % 16
        src, dst = m2_copy(i)
        send(src, dst, ss(R_M2), rs(R_M2), zl, seq_of(i // 4, i % 4, zh, c)).start()

    src, dst = m2_copy(col)
    pltpu.make_async_copy(src, dst, rs(R_M2)).start()

    wait_for(w_buf.at[0, pl.ds(0, 12)], rs(R_W))

    def w_fwd(j):
        rows = w_buf.at[c, pl.ds((y + j) % 4 * 4, 4)]
        return send(rows, rows, ss(R_WSIB), rs(R_WSIB), zl, sib)

    for j in range(1, 4):
        w_fwd(j).start()

    ranks = jnp.concatenate(
        [
            lax.dot_general(
                down_all[adapter[i]], m1[i], (((0,), (0,)), ((), ())), preferred_element_type=F32
            )
            * guide[i]
            for i in range(4)
        ],
        axis=0,
    )
    lr[...] = jnp.transpose(ranks).astype(BF16)

    def lr_copy(i):
        src = lr.at[pl.ds(pl.multiple_of(i * 32, 32), 32)]
        return src, lr_got.at[col]

    @pl.loop(1, 16)
    def _(j):
        i = (col + j) % 16
        src, dst = lr_copy(i)
        send(src, dst, ss(R_LR), rs(R_LR), zl, seq_of(i // 4, i % 4, zh, c)).start()

    src, dst = lr_copy(col)
    pltpu.make_async_copy(src, dst, rs(R_LR)).start()

    wait_for(w_buf.at[0], rs(R_WSIB))
    wait_for(m2, rs(R_M2))
    rows = jnp.transpose(m2[...].reshape(1280, 128).astype(F32)).astype(BF16)
    def project(half):
        p_out[:, 640 * half : 640 * (half + 1)] = jnp.dot(
            rows, w_buf[half].reshape(1280, 640), preferred_element_type=F32
        ).astype(BF16)

    def p_copy(i, half):
        x2 = 2 * c + i // 4
        z2 = i % 4
        src = p_out.at[pl.ds(pl.multiple_of(i * 16, 16), 16), pl.ds(640 * half, 640)]
        dst = p_got.at[zh, :, pl.ds(pl.multiple_of(640 * x, 128), 640)]
        here = jnp.logical_and(jnp.logical_and(x2 == x, z2 == zh), zl == half)
        return src, dst, seq_of(y, x2, z2, zl), jnp.logical_and(here, c == zl)

    def p_start(half):
        @pl.loop(0, 8)
        def _(i):
            src, dst, to, mine = p_copy(i, half)

            @pl.when(mine)
            def _():
                pltpu.make_async_copy(src, dst, rs(R_P)).start()

            @pl.when(jnp.logical_not(mine))
            def _():
                send(src, dst, ss(R_P), rs(R_P), half, to).start()

    project(0)
    p_start(0)
    project(1)
    p_start(1)

    wait_for(lr_got, rs(R_LR))
    low = lr_got[0].astype(F32)
    for i in range(1, 16):
        low = low + lr_got[i].astype(F32)
    lr_sum[...] = low.astype(BF16)

    def lrf_copy(i):
        x2 = 2 * c + x // 2
        z2 = 2 * (x % 2) + i // 2
        zl2 = i % 2
        src = lr_sum.at[pl.ds(pl.multiple_of((i // 2) * 16, 16), 16)]
        dst = lr_fin.at[zh]
        here = jnp.logical_and(jnp.logical_and(x2 == x, z2 == zh), zl2 == zl)
        return src, dst, zl2, seq_of(y, x2, z2, zl), jnp.logical_and(here, c == zl)

    @pl.loop(0, 4)
    def _(i):
        src, dst, zl2, to, mine = lrf_copy(i)

        @pl.when(mine)
        def _():
            pltpu.make_async_copy(src, dst, rs(R_LRF)).start()

        @pl.when(jnp.logical_not(mine))
        def _():
            send(src, dst, ss(R_LRF), rs(R_LRF), zl2, to).start()

    wait_for(lr_fin, rs(R_LRF))
    low = lr_fin[0].astype(F32)
    for i in range(1, 4):
        low = low + lr_fin[i].astype(F32)
    adapted = jnp.dot(low.astype(BF16), up_cat[...], preferred_element_type=F32)
    wait_for(p_got, rs(R_P))
    for i in range(4):
        adapted = adapted + p_got[i].astype(F32)
    out[...] = adapted

    for copy in sib_copies:
        copy.wait_send()
    wait_for(left.at[:, pl.ds(0, 15)], ss(R_LEFT))
    wait_for(left_q.at[pl.ds(0, 15)], ss(R_LEFTQ))

    @pl.when(x != y)
    def _():
        left_q_far.wait_send()

    wait_for(main.at[pl.ds(1, 2), pl.ds(0, 63)], ss(R_MAIN))
    wait_for(main.at[0, pl.ds(0, 63)], ss(R_Q))
    wait_for(w_buf.at[0, pl.ds(0, 3)], ss(R_WX))
    wait_for(w_buf.at[0, pl.ds(0, 12)], ss(R_W))
    wait_for(left.at[:, pl.ds(0, 48)], ss(R_AG))
    ag_sib.wait_send()
    kv_sib.wait_send()
    wait_for(w_buf.at[0], ss(R_WSIB))

    @pl.loop(0, 4)
    def _(tile):
        m1_each(tile, m1_wait_send)

    @pl.loop(0, 4)
    def _(i):
        m1_left_wait_send(i)

    wait_for(m2.at[pl.ds(0, 15)], ss(R_M2))
    wait_for(lr_got.at[pl.ds(0, 15)], ss(R_LR))

    for half in range(2):

        @pl.loop(0, 8)
        def _(i):
            src, dst, to, mine = p_copy(i, half)

            @pl.when(jnp.logical_not(mine))
            def _():
                send(src, dst, ss(R_P), rs(R_P), half, to).wait_send()

    @pl.loop(0, 4)
    def _(i):
        src, dst, zl2, to, mine = lrf_copy(i)

        @pl.when(jnp.logical_not(mine))
        def _():
            send(src, dst, ss(R_LRF), rs(R_LRF), zl2, to).wait_send()


def shards(q, k, v, w, down, up, adapter, weight_eighths, gate_offset, timestep):
    whole = pl.BlockSpec(memory_space=pl.ANY)
    smem = pl.BlockSpec(memory_space=pltpu.SMEM)
    vm = pltpu.VMEM
    mixture = pl.pallas_call(
        body,
        out_shape=jax.ShapeDtypeStruct((16, 2560), F32),
        in_specs=[smem, smem] + [whole] * 6,
        out_specs=pl.BlockSpec(memory_space=pltpu.VMEM),
        scratch_shapes=[
            vm((3, 2, 16, 5120), BF16),
            vm((40, 5120), BF16),
            vm((4, 40, 640), BF16),
            vm((4, 80, 640), BF16),
            vm((2, 16, 80, 640), BF16),
            vm((4, 40, 64), BF16),
            vm((4, 40, 64), BF16),
            vm((4, 80, 64), BF16),
            vm((4, 64, 2560), BF16),
            vm((256, 2560), BF16),
            vm((3, 64, 16, 128), BF16),
            vm((2, 64, 16, 128), BF16),
            vm((16, 16, 128), BF16),
            vm((2, 64, 16, 128), BF16),
            vm((2, 64, 16, 128), BF16),
            vm((128, 1280), BF16),
            vm((4, 80, 512), BF16),
            vm((80, 512), BF16),
            vm((16, 80, 128), BF16),
            vm((512, 256), BF16),
            vm((16, 32, 256), BF16),
            vm((32, 256), BF16),
            vm((128, 1280), BF16),
            vm((4, 16, 2560), BF16),
            vm((4, 16, 256), BF16),
            pltpu.SemaphoreType.DMA((6,)),
            pltpu.SemaphoreType.DMA((17,)),
            pltpu.SemaphoreType.DMA((21,)),
            pltpu.SemaphoreType.REGULAR,
        ],
        compiler_params=pltpu.CompilerParams(
            collective_id=0, has_side_effects=True, vmem_limit_bytes=62 * 2**20
        ),
        name="guided_attention",
    )(adapter, weight_eighths, q, k, v, w, down, up)

    columns = lax.axis_index("branch") * 2560 + jnp.arange(2560, dtype=jnp.int32)
    frequency = jnp.exp((columns % 2560).astype(F32) * (-math.log(10000.0) / 2560))
    angles = timestep.astype(F32)[0] * frequency
    gate_row = gate_offset + jnp.where(columns < 2560, jnp.cos(angles), jnp.sin(angles))
    return (mixture * gate_row[None, :]).astype(BF16)


def solution(mesh):
    placed = (
        P("branch", "seq", None),
        P("branch", "seq", None),
        P("branch", "seq", None),
        P("seq", None),
        P(None, "seq", None),
        P(),
        P(),
        P(),
        P("branch"),
        P(),
    )
    return jax.shard_map(
        shards, mesh=mesh, in_specs=placed, out_specs=P("seq", "branch"), check_vma=False
    )
```

```python
import math

import jax
import jax.numpy as jnp
from jax import lax
from jax.experimental import pallas as pl
from jax.experimental.pallas import tpu as pltpu
from jax.sharding import PartitionSpec as P

MESH = pl.DeviceIdType.MESH
BF16 = jnp.bfloat16
F32 = jnp.float32
HEAD_DIM = 128
GUIDE_UNIT = 0.125
SCORE_SCALE = HEAD_DIM**-0.5 * math.log2(math.e)


def seq_of(y, x, zh, c):
    return ((y * 4 + x) * 4 + zh) * 2 + c


def wait_for(ref, sem):
    pltpu.make_async_copy(ref, ref, sem).wait()


def send(src, dst, send_sem, recv_sem, zl, s):
    return pltpu.make_async_remote_copy(
        src_ref=src, dst_ref=dst, send_sem=send_sem, recv_sem=recv_sem, device_id=(zl, s), device_id_type=MESH
    )


def body(
    adapter,
    weight_eighths,
    timestep,
    gate_offset,
    q_in,
    k_in,
    v_in,
    w_in,
    down_in,
    up_in,
    out,
    qkv_st,
    w_v,
    w_sib,
    w_st,
    w_buf,
    down_v,
    down_sib,
    down_all,
    up_v,
    up_cat,
    main,
    main_sib,
    left_q,
    left,
    left_sib,
    o_t,
    m1,
    mx,
    m2,
    lr,
    lr_got,
    lr_sum,
    p_out,
    p_got,
    lr_fin,
    gate,
    in_sem,
    send_sem,
    recv_sem,
    token,
):
    s = lax.axis_index("seq")
    zl = lax.axis_index("branch")
    c = s % 2
    chip = s // 2
    zh = chip % 4
    x = (chip // 4) % 4
    y = chip // 16
    col = chip // 4
    sib = s + 1 - 2 * c
    slot_left = (x // 2) * 8 + (x % 2) * 4 + zh
    slot = (x // 2) * 32 + y * 8 + (x % 2) * 4 + zh
    (
        R_SIBW,
        R_LEFT,
        R_LEFTQ,
        R_MAIN,
        R_Q,
        R_AG,
        R_AGSIB,
        R_KVSIB,
        R_W,
        R_WSIB,
        R_M1,
        R_M2,
        R_LR,
        R_P,
        R_LRF,
        R_SIBD,
        R_WX,
        R_QS,
    ) = range(18)

    def rs(i):
        return recv_sem.at[i]

    def ss(i):
        return send_sem.at[i]

    loads = [
        pltpu.make_async_copy(w_in, w_v, in_sem.at[0]),
        pltpu.make_async_copy(down_in, down_v, in_sem.at[1]),
        pltpu.make_async_copy(k_in, qkv_st.at[1], in_sem.at[2]),
        pltpu.make_async_copy(v_in, qkv_st.at[2], in_sem.at[3]),
        pltpu.make_async_copy(q_in, qkv_st.at[0], in_sem.at[4]),
        pltpu.make_async_copy(up_in.at[:, :, pl.ds(pl.multiple_of(zl * 2560, 2560), 2560)], up_v, in_sem.at[5]),
        pltpu.make_async_copy(gate_offset, gate.at[0], in_sem.at[6]),
    ]
    for load in loads:
        load.start()


    barrier = pltpu.get_barrier_semaphore()

    @pl.loop(1, 64, unroll=9)
    def _(i):
        pl.semaphore_signal(barrier, 1, device_id=(zl, ((chip + i) % 64) * 2 + c), device_id_type=MESH)

    pl.semaphore_signal(barrier, 1, device_id=(zl, sib), device_id_type=MESH)
    pl.semaphore_signal(barrier, 1, device_id=(1 - zl, s), device_id_type=MESH)
    for load in loads[:5]:
        load.wait()
    pl.semaphore_wait(barrier, 65)

    sib_copies = [
        send(
            w_v.at[:, pl.ds(pl.multiple_of(640 * i + 2560 * (1 - c), 128), 640)],
            w_sib.at[i],
            ss(R_SIBW),
            rs(R_SIBW),
            zl,
            sib,
        )
        for i in range(4)
    ]
    sib_copies.append(send(down_v, down_sib, ss(R_SIBD), rs(R_SIBD), zl, sib))
    for copy in sib_copies:
        copy.start()

    wait_for(w_sib, rs(R_SIBW))
    wait_for(down_sib, rs(R_SIBD))
    pl.semaphore_signal(token, 1, device_id=(1 - zl, s), device_id_type=MESH)

    def joined(own, other):
        first = jnp.where(c == 0, own, other)
        second = jnp.where(c == 0, other, own)
        return jnp.concatenate([first, second], axis=0).astype(BF16)

    for i in range(4):
        own = w_v[:, pl.ds(pl.multiple_of(640 * i + 2560 * c, 128), 640)].astype(F32)
        w_st[i] = joined(own, w_sib[i].astype(F32))
    for j in range(1, 4):
        i = (x + j) % 4
        send(w_st.at[i], w_buf.at[c, col], ss(R_WX), rs(R_WX), zl, seq_of(y, i, zh, c)).start()
    pltpu.make_async_copy(w_st.at[x], w_buf.at[c, col], rs(R_WX)).start()

    def left_copy(i):
        y2 = i // 4
        z2 = i % 4
        head = 5 * (2 * y2 + z2 // 2) + 2
        lanes = pl.ds(pl.multiple_of(head * 128, 128), 128)
        pair = z2 % 2
        return (
            (qkv_st.at[pl.ds(1, 2), pair, :, lanes], left.at[:, x * 16 + y * 4 + zh], R_LEFT),
            (qkv_st.at[0, pair, :, lanes], left_q.at[slot_left], R_LEFTQ),
        )

    @pl.loop(1, 16)
    def _(j):
        i = (y * 4 + zh + j) % 16
        (src, dst, n), (src_q, dst_q, n_q) = left_copy(i)
        send(src, dst, ss(n), rs(n), zl, seq_of(i // 4, x, i % 4, c)).start()
        send(src_q, dst_q, ss(n_q), rs(n_q), zl, seq_of(i // 4, y, i % 4, c)).start()

    (src, dst, n), (src_q, dst_q, n_q) = left_copy(y * 4 + zh)
    pltpu.make_async_copy(src, dst, rs(n)).start()
    left_q_far = send(src_q, dst_q, ss(n_q), rs(n_q), zl, seq_of(y, y, zh, c))

    @pl.when(x == y)
    def _():
        pltpu.make_async_copy(src_q, dst_q, rs(n_q)).start()

    @pl.when(x != y)
    def _():
        left_q_far.start()

    def main_copy(i):
        y2 = i // 16
        x2 = (i // 4) % 4
        z2 = i % 4
        head = 5 * (2 * y2 + x2 // 2) + 3 * (x2 % 2) + z2 // 2
        lanes = pl.ds(pl.multiple_of(head * 128, 128), 128)
        pair = z2 % 2
        return (
            (qkv_st.at[pl.ds(1, 2), pair, :, lanes], main.at[pl.ds(1, 2), slot]),
            (qkv_st.at[0, pair, :, lanes], main.at[0, slot]),
        )

    def kv_start(j):
        i = (chip + j) % 64
        src, dst = main_copy(i)[0]
        send(src, dst, ss(R_MAIN), rs(R_MAIN), zl, i * 2 + c).start()

    @pl.loop(1, 50)
    def _(j):
        kv_start(j)

    slab = left.at[:, pl.ds(x * 16, 16)]
    wait_for(slab, rs(R_LEFT))
    for j in range(1, 4):
        send(slab, slab, ss(R_AG), rs(R_AG), zl, seq_of(y, (x + j) % 4, zh, c)).start()

    @pl.loop(50, 64)
    def _(j):
        kv_start(j)

    src, dst = main_copy(chip)[0]
    pltpu.make_async_copy(src, dst, rs(R_MAIN)).start()

    def flip(a, bit):
        return (a + bit) % 2

    def query_start(i):
        x2 = 2 * flip(x // 2, i // 32) + flip(x % 2, (i // 4) % 2)
        y2 = 2 * flip(y // 2, (i // 16) % 2) + flip(y % 2, (i // 8) % 2)
        to = (y2 * 4 + x2) * 4 + (zh + i) % 4
        src, dst = main_copy(to)[1]
        send(src, dst, ss(R_Q), rs(R_QS + i // 16), zl, to * 2 + c).start()

    src, dst = main_copy(chip)[1]
    pltpu.make_async_copy(src, dst, rs(R_QS)).start()

    w_slab = w_buf.at[c, pl.ds(y * 4, 4)]
    wait_for(w_slab, rs(R_WX))
    w_own_fwd = send(w_slab, w_slab, ss(R_WSIB), rs(R_WSIB), zl, sib)
    w_own_fwd.start()

    @pl.loop(1, 64)
    def _(i):
        query_start(i)

    for j in range(1, 4):
        send(w_slab, w_slab, ss(R_W), rs(R_W), zl, seq_of((y + j) % 4, x, zh, c)).start()

    for i in range(4):
        down_all[i] = joined(down_v[i].astype(F32), down_sib[i].astype(F32))
    loads[5].wait()
    place = lax.broadcasted_iota(jnp.int32, (1, 2560), 1).astype(F32)
    angles = timestep[0].astype(F32) * jnp.exp(place * (-math.log(10000.0) / 2560))
    loads[6].wait()
    gate[...] = gate[...] + jnp.where(zl == 0, jnp.cos(angles), jnp.sin(angles))
    for i in range(4):
        up_cat[64 * i : 64 * (i + 1), :] = up_v[adapter[i]]

    wait_for(left_q, rs(R_LEFTQ))
    wait_for(left.at[:, pl.ds(0, 48)], rs(R_AG))
    ag_sib = send(left, left_sib, ss(R_AGSIB), rs(R_AGSIB), zl, sib)
    ag_sib.start()
    main_kv = main.at[pl.ds(1, 2)]
    wait_for(main_kv, rs(R_MAIN))
    kv_sib = send(main_kv, main_sib, ss(R_KVSIB), rs(R_KVSIB), zl, sib)
    kv_sib.start()
    wait_for(left_sib, rs(R_AGSIB))

    def attend(q, keys, values, tile):
        q = q.reshape(256, 128)
        scores = [
            lax.dot_general(q, k.reshape(1024, 128), (((1,), (1,)), ((), ())), preferred_element_type=F32)
            * SCORE_SCALE
            for k in keys
        ]
        top = jnp.maximum(
            jnp.max(scores[0], axis=1, keepdims=True), jnp.max(scores[1], axis=1, keepdims=True)
        )
        total = 0.0
        mixed = 0.0
        for half in range(2):
            weights = jnp.exp2(scores[half] - top)
            total = total + jnp.sum(weights, axis=1, keepdims=True)
            mixed = mixed + jnp.dot(
                weights.astype(BF16), values[half].reshape(1024, 128), preferred_element_type=F32
            )
        o_t[:, pl.ds(pl.multiple_of(tile * 256, 256), 256)] = jnp.transpose(mixed / total).astype(BF16)

    def attend_main(tile):
        attend(main[0, pl.ds(tile * 16, 16)], (main[1], main_sib[0]), (main[2], main_sib[1]), tile)

    places = (
        ((0, 0), ((0, 80, 0, 0), (80, 48, 1, 0))),
        ((0, 1), ((0, 32, 1, 48), (32, 80, 2, 0), (112, 16, 3, 0))),
        ((1, 0), ((0, 16, 0, 64), (16, 80, 1, 0), (96, 32, 2, 0))),
        ((1, 1), ((0, 48, 2, 32), (48, 80, 3, 0))),
    )
    pair_all = 2 * zl + zh % 2

    def m1_each(tile, action):
        core2 = tile // 2
        lanes = pl.ds(pl.multiple_of((tile % 2) * 256, 256), 256)
        for (odd, which), pieces in places:

            @pl.when(jnp.logical_and(x % 2 == odd, zh // 2 == which))
            def _():
                for first, count, z2, row in pieces:
                    src = o_t.at[pl.ds(first, count), pl.ds(pl.multiple_of(tile * 256, 256), 256)]
                    dst = m1.at[pair_all, pl.ds(row, count), lanes]
                    mine = jnp.logical_and(jnp.logical_and(z2 == zh, c == zl), core2 == c)
                    action(src, dst, mine, seq_of(y, x, z2, core2))

    def m1_start(src, dst, mine, to):
        @pl.when(mine)
        def _():
            pltpu.make_async_copy(src, dst, rs(R_M1)).start()

        @pl.when(jnp.logical_not(mine))
        def _():
            send(src, dst, ss(R_M1), rs(R_M1), c, to).start()

    def m1_wait_send(src, dst, mine, to):
        @pl.when(jnp.logical_not(mine))
        def _():
            send(src, dst, ss(R_M1), rs(R_M1), c, to).wait_send()

    def m1_left_copy(i):
        odd = i % 2
        core2 = i // 2
        src = o_t.at[
            pl.ds(pl.multiple_of(odd * 64, 16), 64), pl.ds(pl.multiple_of(1024 + core2 * 128, 128), 128)
        ]
        dst = m1.at[
            pair_all, pl.ds(pl.multiple_of(16 * (1 - odd), 16), 64), pl.ds(pl.multiple_of(x * 128, 128), 128)
        ]
        return src, dst, 2 * (zh // 2) + odd, 3 * (1 - odd), core2

    def left_mine(x2, z2, core2):
        here = jnp.logical_and(x2 == x, z2 == zh)
        return jnp.logical_and(here, jnp.logical_and(c == zl, core2 == c))

    def m1_left_start(i):
        src, dst, x2, z2, core2 = m1_left_copy(i)
        mine = left_mine(x2, z2, core2)

        @pl.when(mine)
        def _():
            pltpu.make_async_copy(src, dst, rs(R_M1)).start()

        @pl.when(jnp.logical_not(mine))
        def _():
            send(src, dst, ss(R_M1), rs(R_M1), c, seq_of(y, x2, z2, core2)).start()

    def m1_left_wait_send(i):
        src, dst, x2, z2, core2 = m1_left_copy(i)

        @pl.when(jnp.logical_not(left_mine(x2, z2, core2)))
        def _():
            send(src, dst, ss(R_M1), rs(R_M1), c, seq_of(y, x2, z2, core2)).wait_send()

    pl.semaphore_wait(token, 1)
    attend(left_q[...], (left[0], left_sib[0]), (left[1], left_sib[1]), 4)

    @pl.loop(0, 4)
    def _(i):
        m1_left_start(i)

    wait_for(main_sib, rs(R_KVSIB))

    @pl.loop(0, 4)
    def _(t):
        tile = 2 * flip(x // 2, t // 2) + flip(y // 2, t % 2)
        wait_for(main.at[0, pl.ds(0, 16)], rs(R_QS + t))
        attend_main(tile)

        m1_each(tile, m1_start)

    wait_for(m1, rs(R_M1))
    guide = [weight_eighths[i].astype(F32) * GUIDE_UNIT for i in range(4)]
    total = m1[0].astype(F32) * guide[0]
    for i in range(1, 4):
        total = total + m1[i].astype(F32) * guide[i]
    mx[...] = total.astype(BF16)

    def m2_copy(i):
        src = mx.at[:, pl.ds(pl.multiple_of((i // 4) * 128, 128), 128)]
        return src, m2.at[col]

    @pl.loop(1, 16)
    def _(j):
        i = (col + j) % 16
        src, dst = m2_copy(i)
        send(src, dst, ss(R_M2), rs(R_M2), zl, seq_of(i // 4, i % 4, zh, c)).start()

    src, dst = m2_copy(col)
    pltpu.make_async_copy(src, dst, rs(R_M2)).start()

    wait_for(w_buf.at[0, pl.ds(0, 12)], rs(R_W))

    def w_fwd(j):
        rows = w_buf.at[c, pl.ds((y + j) % 4 * 4, 4)]
        return send(rows, rows, ss(R_WSIB), rs(R_WSIB), zl, sib)

    for j in range(1, 4):
        w_fwd(j).start()

    ranks = jnp.concatenate(
        [
            lax.dot_general(
                down_all[adapter[i]], m1[i], (((0,), (0,)), ((), ())), preferred_element_type=F32
            )
            * guide[i]
            for i in range(4)
        ],
        axis=0,
    )
    lr[...] = jnp.transpose(ranks).astype(BF16)

    def lr_copy(i):
        src = lr.at[pl.ds(pl.multiple_of(i * 32, 32), 32)]
        return src, lr_got.at[col]

    @pl.loop(1, 16)
    def _(j):
        i = (col + j) % 16
        src, dst = lr_copy(i)
        send(src, dst, ss(R_LR), rs(R_LR), zl, seq_of(i // 4, i % 4, zh, c)).start()

    src, dst = lr_copy(col)
    pltpu.make_async_copy(src, dst, rs(R_LR)).start()

    wait_for(w_buf.at[0], rs(R_WSIB))
    wait_for(m2, rs(R_M2))
    rows = jnp.transpose(m2[...].reshape(1280, 128).astype(F32)).astype(BF16)
    def project(half):
        p_out[:, 640 * half : 640 * (half + 1)] = jnp.dot(
            rows, w_buf[half].reshape(1280, 640), preferred_element_type=F32
        ).astype(BF16)

    def p_copy(i, half):
        x2 = 2 * c + i // 4
        z2 = i % 4
        src = p_out.at[pl.ds(pl.multiple_of(i * 16, 16), 16), pl.ds(640 * half, 640)]
        dst = p_got.at[zh, :, pl.ds(pl.multiple_of(640 * x, 128), 640)]
        here = jnp.logical_and(jnp.logical_and(x2 == x, z2 == zh), zl == half)
        return src, dst, seq_of(y, x2, z2, zl), jnp.logical_and(here, c == zl)

    def p_start(half):
        @pl.loop(0, 8)
        def _(i):
            src, dst, to, mine = p_copy(i, half)

            @pl.when(mine)
            def _():
                pltpu.make_async_copy(src, dst, rs(R_P)).start()

            @pl.when(jnp.logical_not(mine))
            def _():
                send(src, dst, ss(R_P), rs(R_P), half, to).start()

    project(0)
    p_start(0)
    project(1)
    p_start(1)

    wait_for(lr_got, rs(R_LR))
    low = lr_got[0].astype(F32)
    for i in range(1, 16):
        low = low + lr_got[i].astype(F32)
    lr_sum[...] = low.astype(BF16)

    def lrf_copy(i):
        x2 = 2 * c + x // 2
        z2 = 2 * (x % 2) + i // 2
        zl2 = i % 2
        src = lr_sum.at[pl.ds(pl.multiple_of((i // 2) * 16, 16), 16)]
        dst = lr_fin.at[zh]
        here = jnp.logical_and(jnp.logical_and(x2 == x, z2 == zh), zl2 == zl)
        return src, dst, zl2, seq_of(y, x2, z2, zl), jnp.logical_and(here, c == zl)

    @pl.loop(0, 4)
    def _(i):
        src, dst, zl2, to, mine = lrf_copy(i)

        @pl.when(mine)
        def _():
            pltpu.make_async_copy(src, dst, rs(R_LRF)).start()

        @pl.when(jnp.logical_not(mine))
        def _():
            send(src, dst, ss(R_LRF), rs(R_LRF), zl2, to).start()

    wait_for(lr_fin, rs(R_LRF))
    low = lr_fin[0].astype(F32)
    for i in range(1, 4):
        low = low + lr_fin[i].astype(F32)
    adapted = jnp.dot(low.astype(BF16), up_cat[...], preferred_element_type=F32)
    wait_for(p_got, rs(R_P))
    for i in range(4):
        adapted = adapted + p_got[i].astype(F32)
    out[...] = (adapted * gate[...]).astype(BF16)

    for copy in sib_copies:
        copy.wait_send()
    wait_for(left.at[:, pl.ds(0, 15)], ss(R_LEFT))
    wait_for(left_q.at[pl.ds(0, 15)], ss(R_LEFTQ))

    @pl.when(x != y)
    def _():
        left_q_far.wait_send()

    wait_for(main.at[pl.ds(1, 2), pl.ds(0, 63)], ss(R_MAIN))
    wait_for(main.at[0, pl.ds(0, 63)], ss(R_Q))
    wait_for(w_buf.at[0, pl.ds(0, 3)], ss(R_WX))
    wait_for(w_buf.at[0, pl.ds(0, 12)], ss(R_W))
    wait_for(left.at[:, pl.ds(0, 48)], ss(R_AG))
    ag_sib.wait_send()
    kv_sib.wait_send()
    wait_for(w_buf.at[0], ss(R_WSIB))

    @pl.loop(0, 4)
    def _(tile):
        m1_each(tile, m1_wait_send)

    @pl.loop(0, 4)
    def _(i):
        m1_left_wait_send(i)

    wait_for(m2.at[pl.ds(0, 15)], ss(R_M2))
    wait_for(lr_got.at[pl.ds(0, 15)], ss(R_LR))

    for half in range(2):

        @pl.loop(0, 8)
        def _(i):
            src, dst, to, mine = p_copy(i, half)

            @pl.when(jnp.logical_not(mine))
            def _():
                send(src, dst, ss(R_P), rs(R_P), half, to).wait_send()

    @pl.loop(0, 4)
    def _(i):
        src, dst, zl2, to, mine = lrf_copy(i)

        @pl.when(jnp.logical_not(mine))
        def _():
            send(src, dst, ss(R_LRF), rs(R_LRF), zl2, to).wait_send()


def shards(q, k, v, w, down, up, adapter, weight_eighths, gate_offset, timestep):
    whole = pl.BlockSpec(memory_space=pl.ANY)
    smem = pl.BlockSpec(memory_space=pltpu.SMEM)
    vm = pltpu.VMEM
    return pl.pallas_call(
        body,
        out_shape=jax.ShapeDtypeStruct((16, 2560), BF16),
        in_specs=[smem] * 3 + [whole] * 7,
        out_specs=pl.BlockSpec(memory_space=pltpu.VMEM),
        scratch_shapes=[
            vm((3, 2, 16, 5120), BF16),
            vm((40, 5120), BF16),
            vm((4, 40, 640), BF16),
            vm((4, 80, 640), BF16),
            vm((2, 16, 80, 640), BF16),
            vm((4, 40, 64), BF16),
            vm((4, 40, 64), BF16),
            vm((4, 80, 64), BF16),
            vm((4, 64, 2560), BF16),
            vm((256, 2560), BF16),
            vm((3, 64, 16, 128), BF16),
            vm((2, 64, 16, 128), BF16),
            vm((16, 16, 128), BF16),
            vm((2, 64, 16, 128), BF16),
            vm((2, 64, 16, 128), BF16),
            vm((128, 1280), BF16),
            vm((4, 80, 512), BF16),
            vm((80, 512), BF16),
            vm((16, 80, 128), BF16),
            vm((512, 256), BF16),
            vm((16, 32, 256), BF16),
            vm((32, 256), BF16),
            vm((128, 1280), BF16),
            vm((4, 16, 2560), BF16),
            vm((4, 16, 256), BF16),
            vm((1, 2560), F32),
            pltpu.SemaphoreType.DMA((7,)),
            pltpu.SemaphoreType.DMA((17,)),
            pltpu.SemaphoreType.DMA((21,)),
            pltpu.SemaphoreType.REGULAR,
        ],
        compiler_params=pltpu.CompilerParams(
            collective_id=0, has_side_effects=True, vmem_limit_bytes=62 * 2**20
        ),
        name="guided_attention",
    )(adapter, weight_eighths, timestep, gate_offset, q, k, v, w, down, up)


def solution(mesh):
    placed = (
        P("branch", "seq", None),
        P("branch", "seq", None),
        P("branch", "seq", None),
        P("seq", None),
        P(None, "seq", None),
        P(),
        P(),
        P(),
        P("branch"),
        P(),
    )
    return jax.shard_map(
        shards, mesh=mesh, in_specs=placed, out_specs=P("seq", "branch"), check_vma=False
    )
```

```python
import math

import jax
import jax.numpy as jnp
from jax import lax
from jax.experimental import pallas as pl
from jax.experimental.pallas import tpu as pltpu
from jax.sharding import PartitionSpec as P

MESH = pl.DeviceIdType.MESH
BF16 = jnp.bfloat16
F32 = jnp.float32
HEAD_DIM = 128
GUIDE_UNIT = 0.125
SCORE_SCALE = HEAD_DIM**-0.5 * math.log2(math.e)


def seq_of(y, x, zh, c):
    return ((y * 4 + x) * 4 + zh) * 2 + c


def wait_for(ref, sem):
    pltpu.make_async_copy(ref, ref, sem).wait()


def send(src, dst, send_sem, recv_sem, zl, s):
    return pltpu.make_async_remote_copy(
        src_ref=src, dst_ref=dst, send_sem=send_sem, recv_sem=recv_sem, device_id=(zl, s), device_id_type=MESH
    )


def body(
    adapter,
    weight_eighths,
    timestep,
    gate_offset,
    q_in,
    k_in,
    v_in,
    w_in,
    down_in,
    up_in,
    out,
    qkv_st,
    w_v,
    w_sib,
    w_st,
    w_buf,
    down_v,
    down_sib,
    down_all,
    up_v,
    up_cat,
    main,
    main_sib,
    left_q,
    left,
    left_sib,
    o_t,
    m1,
    mx,
    m2,
    lr,
    lr_got,
    lr_sum,
    p_out,
    p_got,
    lr_fin,
    gate,
    in_sem,
    send_sem,
    recv_sem,
    token,
):
    s = lax.axis_index("seq")
    zl = lax.axis_index("branch")
    c = s % 2
    chip = s // 2
    zh = chip % 4
    x = (chip // 4) % 4
    y = chip // 16
    col = chip // 4
    sib = s + 1 - 2 * c
    slot_left = (x // 2) * 8 + (x % 2) * 4 + zh
    slot = (x // 2) * 32 + y * 8 + (x % 2) * 4 + zh
    (
        R_SIBW,
        R_LEFT,
        R_LEFTQ,
        R_MAIN,
        R_Q,
        R_AG,
        R_AGSIB,
        R_KVSIB,
        R_W,
        R_WSIB,
        R_M1,
        R_M2,
        R_LR,
        R_P,
        R_LRF,
        R_SIBD,
        R_WX,
        R_QS,
    ) = range(18)

    def rs(i):
        return recv_sem.at[i]

    def ss(i):
        return send_sem.at[i]

    loads = [
        pltpu.make_async_copy(w_in, w_v, in_sem.at[0]),
        pltpu.make_async_copy(down_in, down_v, in_sem.at[1]),
        pltpu.make_async_copy(k_in, qkv_st.at[1], in_sem.at[2]),
        pltpu.make_async_copy(v_in, qkv_st.at[2], in_sem.at[3]),
        pltpu.make_async_copy(q_in, qkv_st.at[0], in_sem.at[4]),
        pltpu.make_async_copy(up_in.at[:, :, pl.ds(pl.multiple_of(zl * 2560, 2560), 2560)], up_v, in_sem.at[5]),
        pltpu.make_async_copy(gate_offset, gate.at[0], in_sem.at[6]),
    ]
    for load in loads:
        load.start()


    barrier = pltpu.get_barrier_semaphore()

    @pl.loop(1, 64, unroll=9)
    def _(i):
        pl.semaphore_signal(barrier, 1, device_id=(zl, ((chip + i) % 64) * 2 + c), device_id_type=MESH)

    pl.semaphore_signal(barrier, 1, device_id=(zl, sib), device_id_type=MESH)
    pl.semaphore_signal(barrier, 1, device_id=(1 - zl, s), device_id_type=MESH)
    for load in loads[:5]:
        load.wait()
    pl.semaphore_wait(barrier, 65)

    sib_copies = [
        send(
            w_v.at[:, pl.ds(pl.multiple_of(640 * i + 2560 * (1 - c), 128), 640)],
            w_sib.at[i],
            ss(R_SIBW),
            rs(R_SIBW),
            zl,
            sib,
        )
        for i in range(4)
    ]
    sib_copies.append(send(down_v, down_sib, ss(R_SIBD), rs(R_SIBD), zl, sib))
    for copy in sib_copies:
        copy.start()

    def left_copy(i):
        y2 = i // 4
        z2 = i % 4
        head = 5 * (2 * y2 + z2 // 2) + 2
        lanes = pl.ds(pl.multiple_of(head * 128, 128), 128)
        pair = z2 % 2
        return (
            (qkv_st.at[pl.ds(1, 2), pair, :, lanes], left.at[:, x * 16 + y * 4 + zh], R_LEFT),
            (qkv_st.at[0, pair, :, lanes], left_q.at[slot_left], R_LEFTQ),
        )

    @pl.loop(1, 16)
    def _(j):
        i = (y * 4 + zh + j) % 16
        (src, dst, n), (src_q, dst_q, n_q) = left_copy(i)
        send(src, dst, ss(n), rs(n), zl, seq_of(i // 4, x, i % 4, c)).start()
        send(src_q, dst_q, ss(n_q), rs(n_q), zl, seq_of(i // 4, y, i % 4, c)).start()

    (src, dst, n), (src_q, dst_q, n_q) = left_copy(y * 4 + zh)
    pltpu.make_async_copy(src, dst, rs(n)).start()
    left_q_far = send(src_q, dst_q, ss(n_q), rs(n_q), zl, seq_of(y, y, zh, c))

    @pl.when(x == y)
    def _():
        pltpu.make_async_copy(src_q, dst_q, rs(n_q)).start()

    @pl.when(x != y)
    def _():
        left_q_far.start()

    def main_copy(i):
        y2 = i // 16
        x2 = (i // 4) % 4
        z2 = i % 4
        head = 5 * (2 * y2 + x2 // 2) + 3 * (x2 % 2) + z2 // 2
        lanes = pl.ds(pl.multiple_of(head * 128, 128), 128)
        pair = z2 % 2
        return (
            (qkv_st.at[pl.ds(1, 2), pair, :, lanes], main.at[pl.ds(1, 2), slot]),
            (qkv_st.at[0, pair, :, lanes], main.at[0, slot]),
        )

    def kv_start(j):
        i = (chip + j) % 64
        src, dst = main_copy(i)[0]
        send(src, dst, ss(R_MAIN), rs(R_MAIN), zl, i * 2 + c).start()

    @pl.loop(1, 9)
    def _(j):
        kv_start(j)

    wait_for(w_sib, rs(R_SIBW))
    wait_for(down_sib, rs(R_SIBD))
    pl.semaphore_signal(token, 1, device_id=(1 - zl, s), device_id_type=MESH)

    def joined(own, other):
        first = jnp.where(c == 0, own, other)
        second = jnp.where(c == 0, other, own)
        return jnp.concatenate([first, second], axis=0).astype(BF16)

    for i in range(4):
        own = w_v[:, pl.ds(pl.multiple_of(640 * i + 2560 * c, 128), 640)].astype(F32)
        w_st[i] = joined(own, w_sib[i].astype(F32))
    for j in range(1, 4):
        i = (x + j) % 4
        send(w_st.at[i], w_buf.at[c, col], ss(R_WX), rs(R_WX), zl, seq_of(y, i, zh, c)).start()
    pltpu.make_async_copy(w_st.at[x], w_buf.at[c, col], rs(R_WX)).start()

    @pl.loop(9, 50)
    def _(j):
        kv_start(j)

    @pl.loop(50, 64)
    def _(j):
        kv_start(j)

    src, dst = main_copy(chip)[0]
    pltpu.make_async_copy(src, dst, rs(R_MAIN)).start()

    def flip(a, bit):
        return (a + bit) % 2

    def query_start(i):
        x2 = 2 * flip(x // 2, i // 32) + flip(x % 2, (i // 4) % 2)
        y2 = 2 * flip(y // 2, (i // 16) % 2) + flip(y % 2, (i // 8) % 2)
        to = (y2 * 4 + x2) * 4 + (zh + i) % 4
        src, dst = main_copy(to)[1]
        send(src, dst, ss(R_Q), rs(R_QS + i // 16), zl, to * 2 + c).start()

    src, dst = main_copy(chip)[1]
    pltpu.make_async_copy(src, dst, rs(R_QS)).start()

    w_slab = w_buf.at[c, pl.ds(y * 4, 4)]
    wait_for(w_slab, rs(R_WX))
    w_own_fwd = send(w_slab, w_slab, ss(R_WSIB), rs(R_WSIB), zl, sib)
    w_own_fwd.start()

    @pl.loop(1, 16)
    def _(i):
        query_start(i)

    slab = left.at[:, pl.ds(x * 16, 16)]
    wait_for(slab, rs(R_LEFT))
    for j in range(1, 4):
        send(slab, slab, ss(R_AG), rs(R_AG), zl, seq_of(y, (x + j) % 4, zh, c)).start()

    @pl.loop(16, 64)
    def _(i):
        query_start(i)

    for j in range(1, 4):
        send(w_slab, w_slab, ss(R_W), rs(R_W), zl, seq_of((y + j) % 4, x, zh, c)).start()

    for i in range(4):
        down_all[i] = joined(down_v[i].astype(F32), down_sib[i].astype(F32))
    loads[5].wait()
    place = lax.broadcasted_iota(jnp.int32, (1, 2560), 1).astype(F32)
    angles = timestep[0].astype(F32) * jnp.exp(place * (-math.log(10000.0) / 2560))
    loads[6].wait()
    gate[...] = gate[...] + jnp.where(zl == 0, jnp.cos(angles), jnp.sin(angles))
    for i in range(4):
        up_cat[64 * i : 64 * (i + 1), :] = up_v[adapter[i]]

    wait_for(left_q, rs(R_LEFTQ))
    wait_for(left.at[:, pl.ds(0, 48)], rs(R_AG))
    ag_sib = send(left, left_sib, ss(R_AGSIB), rs(R_AGSIB), zl, sib)
    ag_sib.start()
    main_kv = main.at[pl.ds(1, 2)]
    wait_for(main_kv, rs(R_MAIN))
    kv_sib = send(main_kv, main_sib, ss(R_KVSIB), rs(R_KVSIB), zl, sib)
    kv_sib.start()
    wait_for(left_sib, rs(R_AGSIB))

    def attend(q, keys, values, tile):
        q = q.reshape(256, 128)
        scores = [
            lax.dot_general(q, k.reshape(1024, 128), (((1,), (1,)), ((), ())), preferred_element_type=F32)
            * SCORE_SCALE
            for k in keys
        ]
        top = jnp.maximum(
            jnp.max(scores[0], axis=1, keepdims=True), jnp.max(scores[1], axis=1, keepdims=True)
        )
        total = 0.0
        mixed = 0.0
        for half in range(2):
            weights = jnp.exp2(scores[half] - top)
            total = total + jnp.sum(weights, axis=1, keepdims=True)
            mixed = mixed + jnp.dot(
                weights.astype(BF16), values[half].reshape(1024, 128), preferred_element_type=F32
            )
        o_t[:, pl.ds(pl.multiple_of(tile * 256, 256), 256)] = jnp.transpose(mixed / total).astype(BF16)

    def attend_main(tile):
        attend(main[0, pl.ds(tile * 16, 16)], (main[1], main_sib[0]), (main[2], main_sib[1]), tile)

    places = (
        ((0, 0), ((0, 80, 0, 0), (80, 48, 1, 0))),
        ((0, 1), ((0, 32, 1, 48), (32, 80, 2, 0), (112, 16, 3, 0))),
        ((1, 0), ((0, 16, 0, 64), (16, 80, 1, 0), (96, 32, 2, 0))),
        ((1, 1), ((0, 48, 2, 32), (48, 80, 3, 0))),
    )
    pair_all = 2 * zl + zh % 2

    def m1_each(tile, action):
        core2 = tile // 2
        lanes = pl.ds(pl.multiple_of((tile % 2) * 256, 256), 256)
        for (odd, which), pieces in places:

            @pl.when(jnp.logical_and(x % 2 == odd, zh // 2 == which))
            def _():
                for first, count, z2, row in pieces:
                    src = o_t.at[pl.ds(first, count), pl.ds(pl.multiple_of(tile * 256, 256), 256)]
                    dst = m1.at[pair_all, pl.ds(row, count), lanes]
                    mine = jnp.logical_and(jnp.logical_and(z2 == zh, c == zl), core2 == c)
                    action(src, dst, mine, seq_of(y, x, z2, core2))

    def m1_start(src, dst, mine, to):
        @pl.when(mine)
        def _():
            pltpu.make_async_copy(src, dst, rs(R_M1)).start()

        @pl.when(jnp.logical_not(mine))
        def _():
            send(src, dst, ss(R_M1), rs(R_M1), c, to).start()

    def m1_wait_send(src, dst, mine, to):
        @pl.when(jnp.logical_not(mine))
        def _():
            send(src, dst, ss(R_M1), rs(R_M1), c, to).wait_send()

    def m1_left_copy(i):
        odd = i % 2
        core2 = i // 2
        src = o_t.at[
            pl.ds(pl.multiple_of(odd * 64, 16), 64), pl.ds(pl.multiple_of(1024 + core2 * 128, 128), 128)
        ]
        dst = m1.at[
            pair_all, pl.ds(pl.multiple_of(16 * (1 - odd), 16), 64), pl.ds(pl.multiple_of(x * 128, 128), 128)
        ]
        return src, dst, 2 * (zh // 2) + odd, 3 * (1 - odd), core2

    def left_mine(x2, z2, core2):
        here = jnp.logical_and(x2 == x, z2 == zh)
        return jnp.logical_and(here, jnp.logical_and(c == zl, core2 == c))

    def m1_left_start(i):
        src, dst, x2, z2, core2 = m1_left_copy(i)
        mine = left_mine(x2, z2, core2)

        @pl.when(mine)
        def _():
            pltpu.make_async_copy(src, dst, rs(R_M1)).start()

        @pl.when(jnp.logical_not(mine))
        def _():
            send(src, dst, ss(R_M1), rs(R_M1), c, seq_of(y, x2, z2, core2)).start()

    def m1_left_wait_send(i):
        src, dst, x2, z2, core2 = m1_left_copy(i)

        @pl.when(jnp.logical_not(left_mine(x2, z2, core2)))
        def _():
            send(src, dst, ss(R_M1), rs(R_M1), c, seq_of(y, x2, z2, core2)).wait_send()

    pl.semaphore_wait(token, 1)
    attend(left_q[...], (left[0], left_sib[0]), (left[1], left_sib[1]), 4)

    @pl.loop(0, 4)
    def _(i):
        m1_left_start(i)

    wait_for(main_sib, rs(R_KVSIB))

    @pl.loop(0, 4)
    def _(t):
        tile = 2 * flip(x // 2, t // 2) + flip(y // 2, t % 2)
        wait_for(main.at[0, pl.ds(0, 16)], rs(R_QS + t))
        attend_main(tile)

        m1_each(tile, m1_start)

    wait_for(m1, rs(R_M1))
    guide = [weight_eighths[i].astype(F32) * GUIDE_UNIT for i in range(4)]
    total = m1[0].astype(F32) * guide[0]
    for i in range(1, 4):
        total = total + m1[i].astype(F32) * guide[i]
    mx[...] = total.astype(BF16)

    def m2_copy(i):
        src = mx.at[:, pl.ds(pl.multiple_of((i // 4) * 128, 128), 128)]
        return src, m2.at[col]

    @pl.loop(1, 16)
    def _(j):
        i = (col + j) % 16
        src, dst = m2_copy(i)
        send(src, dst, ss(R_M2), rs(R_M2), zl, seq_of(i // 4, i % 4, zh, c)).start()

    src, dst = m2_copy(col)
    pltpu.make_async_copy(src, dst, rs(R_M2)).start()

    wait_for(w_buf.at[0, pl.ds(0, 12)], rs(R_W))

    def w_fwd(j):
        rows = w_buf.at[c, pl.ds((y + j) % 4 * 4, 4)]
        return send(rows, rows, ss(R_WSIB), rs(R_WSIB), zl, sib)

    for j in range(1, 4):
        w_fwd(j).start()

    ranks = jnp.concatenate(
        [
            lax.dot_general(
                down_all[adapter[i]], m1[i], (((0,), (0,)), ((), ())), preferred_element_type=F32
            )
            * guide[i]
            for i in range(4)
        ],
        axis=0,
    )
    lr[...] = jnp.transpose(ranks).astype(BF16)

    def lr_copy(i):
        src = lr.at[pl.ds(pl.multiple_of(i * 32, 32), 32)]
        return src, lr_got.at[col]

    @pl.loop(1, 16)
    def _(j):
        i = (col + j) % 16
        src, dst = lr_copy(i)
        send(src, dst, ss(R_LR), rs(R_LR), zl, seq_of(i // 4, i % 4, zh, c)).start()

    src, dst = lr_copy(col)
    pltpu.make_async_copy(src, dst, rs(R_LR)).start()

    wait_for(w_buf.at[0], rs(R_WSIB))
    wait_for(m2, rs(R_M2))
    rows = jnp.transpose(m2[...].reshape(1280, 128).astype(F32)).astype(BF16)
    def project(half):
        p_out[:, 640 * half : 640 * (half + 1)] = jnp.dot(
            rows, w_buf[half].reshape(1280, 640), preferred_element_type=F32
        ).astype(BF16)

    def p_copy(i, half):
        x2 = 2 * c + i // 4
        z2 = i % 4
        src = p_out.at[pl.ds(pl.multiple_of(i * 16, 16), 16), pl.ds(640 * half, 640)]
        dst = p_got.at[zh, :, pl.ds(pl.multiple_of(640 * x, 128), 640)]
        here = jnp.logical_and(jnp.logical_and(x2 == x, z2 == zh), zl == half)
        return src, dst, seq_of(y, x2, z2, zl), jnp.logical_and(here, c == zl)

    def p_start(half):
        @pl.loop(0, 8)
        def _(i):
            src, dst, to, mine = p_copy(i, half)

            @pl.when(mine)
            def _():
                pltpu.make_async_copy(src, dst, rs(R_P)).start()

            @pl.when(jnp.logical_not(mine))
            def _():
                send(src, dst, ss(R_P), rs(R_P), half, to).start()

    project(0)
    p_start(0)
    project(1)
    p_start(1)

    wait_for(lr_got, rs(R_LR))
    low = lr_got[0].astype(F32)
    for i in range(1, 16):
        low = low + lr_got[i].astype(F32)
    lr_sum[...] = low.astype(BF16)

    def lrf_copy(i):
        x2 = 2 * c + x // 2
        z2 = 2 * (x % 2) + i // 2
        zl2 = i % 2
        src = lr_sum.at[pl.ds(pl.multiple_of((i // 2) * 16, 16), 16)]
        dst = lr_fin.at[zh]
        here = jnp.logical_and(jnp.logical_and(x2 == x, z2 == zh), zl2 == zl)
        return src, dst, zl2, seq_of(y, x2, z2, zl), jnp.logical_and(here, c == zl)

    @pl.loop(0, 4)
    def _(i):
        src, dst, zl2, to, mine = lrf_copy(i)

        @pl.when(mine)
        def _():
            pltpu.make_async_copy(src, dst, rs(R_LRF)).start()

        @pl.when(jnp.logical_not(mine))
        def _():
            send(src, dst, ss(R_LRF), rs(R_LRF), zl2, to).start()

    wait_for(lr_fin, rs(R_LRF))
    low = lr_fin[0].astype(F32)
    for i in range(1, 4):
        low = low + lr_fin[i].astype(F32)
    adapted = jnp.dot(low.astype(BF16), up_cat[...], preferred_element_type=F32)
    wait_for(p_got, rs(R_P))
    for i in range(4):
        adapted = adapted + p_got[i].astype(F32)
    out[...] = (adapted * gate[...]).astype(BF16)

    for copy in sib_copies:
        copy.wait_send()
    wait_for(left.at[:, pl.ds(0, 15)], ss(R_LEFT))
    wait_for(left_q.at[pl.ds(0, 15)], ss(R_LEFTQ))

    @pl.when(x != y)
    def _():
        left_q_far.wait_send()

    wait_for(main.at[pl.ds(1, 2), pl.ds(0, 63)], ss(R_MAIN))
    wait_for(main.at[0, pl.ds(0, 63)], ss(R_Q))
    wait_for(w_buf.at[0, pl.ds(0, 3)], ss(R_WX))
    wait_for(w_buf.at[0, pl.ds(0, 12)], ss(R_W))
    wait_for(left.at[:, pl.ds(0, 48)], ss(R_AG))
    ag_sib.wait_send()
    kv_sib.wait_send()
    wait_for(w_buf.at[0], ss(R_WSIB))

    @pl.loop(0, 4)
    def _(tile):
        m1_each(tile, m1_wait_send)

    @pl.loop(0, 4)
    def _(i):
        m1_left_wait_send(i)

    wait_for(m2.at[pl.ds(0, 15)], ss(R_M2))
    wait_for(lr_got.at[pl.ds(0, 15)], ss(R_LR))

    for half in range(2):

        @pl.loop(0, 8)
        def _(i):
            src, dst, to, mine = p_copy(i, half)

            @pl.when(jnp.logical_not(mine))
            def _():
                send(src, dst, ss(R_P), rs(R_P), half, to).wait_send()

    @pl.loop(0, 4)
    def _(i):
        src, dst, zl2, to, mine = lrf_copy(i)

        @pl.when(jnp.logical_not(mine))
        def _():
            send(src, dst, ss(R_LRF), rs(R_LRF), zl2, to).wait_send()


def shards(q, k, v, w, down, up, adapter, weight_eighths, gate_offset, timestep):
    whole = pl.BlockSpec(memory_space=pl.ANY)
    smem = pl.BlockSpec(memory_space=pltpu.SMEM)
    vm = pltpu.VMEM
    return pl.pallas_call(
        body,
        out_shape=jax.ShapeDtypeStruct((16, 2560), BF16),
        in_specs=[smem] * 3 + [whole] * 7,
        out_specs=pl.BlockSpec(memory_space=pltpu.VMEM),
        scratch_shapes=[
            vm((3, 2, 16, 5120), BF16),
            vm((40, 5120), BF16),
            vm((4, 40, 640), BF16),
            vm((4, 80, 640), BF16),
            vm((2, 16, 80, 640), BF16),
            vm((4, 40, 64), BF16),
            vm((4, 40, 64), BF16),
            vm((4, 80, 64), BF16),
            vm((4, 64, 2560), BF16),
            vm((256, 2560), BF16),
            vm((3, 64, 16, 128), BF16),
            vm((2, 64, 16, 128), BF16),
            vm((16, 16, 128), BF16),
            vm((2, 64, 16, 128), BF16),
            vm((2, 64, 16, 128), BF16),
            vm((128, 1280), BF16),
            vm((4, 80, 512), BF16),
            vm((80, 512), BF16),
            vm((16, 80, 128), BF16),
            vm((512, 256), BF16),
            vm((16, 32, 256), BF16),
            vm((32, 256), BF16),
            vm((128, 1280), BF16),
            vm((4, 16, 2560), BF16),
            vm((4, 16, 256), BF16),
            vm((1, 2560), F32),
            pltpu.SemaphoreType.DMA((7,)),
            pltpu.SemaphoreType.DMA((17,)),
            pltpu.SemaphoreType.DMA((21,)),
            pltpu.SemaphoreType.REGULAR,
        ],
        compiler_params=pltpu.CompilerParams(
            collective_id=0, has_side_effects=True, vmem_limit_bytes=62 * 2**20
        ),
        name="guided_attention",
    )(adapter, weight_eighths, timestep, gate_offset, q, k, v, w, down, up)


def solution(mesh):
    placed = (
        P("branch", "seq", None),
        P("branch", "seq", None),
        P("branch", "seq", None),
        P("seq", None),
        P(None, "seq", None),
        P(),
        P(),
        P(),
        P("branch"),
        P(),
    )
    return jax.shard_map(
        shards, mesh=mesh, in_specs=placed, out_specs=P("seq", "branch"), check_vma=False
    )
```

```python
import math

import jax
import jax.numpy as jnp
from jax import lax
from jax.experimental import pallas as pl
from jax.experimental.pallas import tpu as pltpu
from jax.sharding import PartitionSpec as P

MESH = pl.DeviceIdType.MESH
BF16 = jnp.bfloat16
F32 = jnp.float32
HEAD_DIM = 128
GUIDE_UNIT = 0.125
SCORE_SCALE = HEAD_DIM**-0.5 * math.log2(math.e)


def seq_of(y, x, zh, c):
    return ((y * 4 + x) * 4 + zh) * 2 + c


def wait_for(ref, sem):
    pltpu.make_async_copy(ref, ref, sem).wait()


def send(src, dst, send_sem, recv_sem, zl, s):
    return pltpu.make_async_remote_copy(
        src_ref=src, dst_ref=dst, send_sem=send_sem, recv_sem=recv_sem, device_id=(zl, s), device_id_type=MESH
    )


def body(
    adapter,
    weight_eighths,
    timestep,
    gate_offset,
    q_in,
    k_in,
    v_in,
    w_in,
    down_in,
    up_in,
    out,
    qkv_st,
    w_v,
    w_sib,
    w_st,
    w_buf,
    down_v,
    down_sib,
    down_all,
    up_v,
    up_cat,
    main,
    main_sib,
    left_q,
    left,
    left_sib,
    o_t,
    m1,
    mx,
    m2,
    lr,
    lr_got,
    lr_sum,
    p_out,
    p_got,
    lr_fin,
    gate,
    in_sem,
    send_sem,
    recv_sem,
    token,
):
    s = lax.axis_index("seq")
    zl = lax.axis_index("branch")
    c = s % 2
    chip = s // 2
    zh = chip % 4
    x = (chip // 4) % 4
    y = chip // 16
    col = chip // 4
    sib = s + 1 - 2 * c
    slot_left = (x // 2) * 8 + (x % 2) * 4 + zh
    slot = (x // 2) * 32 + y * 8 + (x % 2) * 4 + zh
    (
        R_SIBW,
        R_LEFT,
        R_LEFTQ,
        R_MAIN,
        R_Q,
        R_AG,
        R_AGSIB,
        R_KVSIB,
        R_W,
        R_WSIB,
        R_M1,
        R_M2,
        R_LR,
        R_P,
        R_LRF,
        R_SIBD,
        R_WX,
        R_QS,
    ) = range(18)

    def rs(i):
        return recv_sem.at[i]

    def ss(i):
        return send_sem.at[i]

    loads = [
        pltpu.make_async_copy(w_in, w_v, in_sem.at[0]),
        pltpu.make_async_copy(down_in, down_v, in_sem.at[1]),
        pltpu.make_async_copy(k_in, qkv_st.at[1], in_sem.at[2]),
        pltpu.make_async_copy(v_in, qkv_st.at[2], in_sem.at[3]),
        pltpu.make_async_copy(q_in, qkv_st.at[0], in_sem.at[4]),
        pltpu.make_async_copy(up_in.at[:, :, pl.ds(pl.multiple_of(zl * 2560, 2560), 2560)], up_v, in_sem.at[5]),
        pltpu.make_async_copy(gate_offset, gate.at[0], in_sem.at[6]),
    ]
    for load in loads:
        load.start()


    barrier = pltpu.get_barrier_semaphore()

    @pl.loop(1, 64, unroll=9)
    def _(i):
        pl.semaphore_signal(barrier, 1, device_id=(zl, ((chip + i) % 64) * 2 + c), device_id_type=MESH)

    pl.semaphore_signal(barrier, 1, device_id=(zl, sib), device_id_type=MESH)
    pl.semaphore_signal(barrier, 1, device_id=(1 - zl, s), device_id_type=MESH)
    for load in loads[:5]:
        load.wait()
    pl.semaphore_wait(barrier, 65)

    sib_copies = [
        send(
            w_v.at[:, pl.ds(pl.multiple_of(640 * i + 2560 * (1 - c), 128), 640)],
            w_sib.at[i],
            ss(R_SIBW),
            rs(R_SIBW),
            zl,
            sib,
        )
        for i in range(4)
    ]
    sib_copies.append(send(down_v, down_sib, ss(R_SIBD), rs(R_SIBD), zl, sib))
    for copy in sib_copies:
        copy.start()

    def left_copy(i):
        y2 = i // 4
        z2 = i % 4
        head = 5 * (2 * y2 + z2 // 2) + 2
        lanes = pl.ds(pl.multiple_of(head * 128, 128), 128)
        pair = z2 % 2
        return (
            (qkv_st.at[pl.ds(1, 2), pair, :, lanes], left.at[:, x * 16 + y * 4 + zh], R_LEFT),
            (qkv_st.at[0, pair, :, lanes], left_q.at[slot_left], R_LEFTQ),
        )

    @pl.loop(1, 16)
    def _(j):
        i = (y * 4 + zh + j) % 16
        (src, dst, n), (src_q, dst_q, n_q) = left_copy(i)
        send(src, dst, ss(n), rs(n), zl, seq_of(i // 4, x, i % 4, c)).start()
        send(src_q, dst_q, ss(n_q), rs(n_q), zl, seq_of(i // 4, y, i % 4, c)).start()

    (src, dst, n), (src_q, dst_q, n_q) = left_copy(y * 4 + zh)
    pltpu.make_async_copy(src, dst, rs(n)).start()
    left_q_far = send(src_q, dst_q, ss(n_q), rs(n_q), zl, seq_of(y, y, zh, c))

    @pl.when(x == y)
    def _():
        pltpu.make_async_copy(src_q, dst_q, rs(n_q)).start()

    @pl.when(x != y)
    def _():
        left_q_far.start()

    def main_copy(i):
        y2 = i // 16
        x2 = (i // 4) % 4
        z2 = i % 4
        head = 5 * (2 * y2 + x2 // 2) + 3 * (x2 % 2) + z2 // 2
        lanes = pl.ds(pl.multiple_of(head * 128, 128), 128)
        pair = z2 % 2
        return (
            (qkv_st.at[pl.ds(1, 2), pair, :, lanes], main.at[pl.ds(1, 2), slot]),
            (qkv_st.at[0, pair, :, lanes], main.at[0, slot]),
        )

    def kv_start(j):
        i = (chip + j) % 64
        src, dst = main_copy(i)[0]
        send(src, dst, ss(R_MAIN), rs(R_MAIN), zl, i * 2 + c).start()

    @pl.loop(1, 9)
    def _(j):
        kv_start(j)

    wait_for(w_sib, rs(R_SIBW))
    wait_for(down_sib, rs(R_SIBD))
    pl.semaphore_signal(token, 1, device_id=(1 - zl, s), device_id_type=MESH)

    def joined(own, other):
        first = jnp.where(c == 0, own, other)
        second = jnp.where(c == 0, other, own)
        return jnp.concatenate([first, second], axis=0).astype(BF16)

    for i in range(4):
        own = w_v[:, pl.ds(pl.multiple_of(640 * i + 2560 * c, 128), 640)].astype(F32)
        w_st[i] = joined(own, w_sib[i].astype(F32))
    for j in range(1, 4):
        i = (x + j) % 4
        send(w_st.at[i], w_buf.at[c, col], ss(R_WX), rs(R_WX), zl, seq_of(y, i, zh, c)).start()
    pltpu.make_async_copy(w_st.at[x], w_buf.at[c, col], rs(R_WX)).start()

    @pl.loop(9, 50)
    def _(j):
        kv_start(j)

    @pl.loop(50, 64)
    def _(j):
        kv_start(j)

    src, dst = main_copy(chip)[0]
    pltpu.make_async_copy(src, dst, rs(R_MAIN)).start()

    def flip(a, bit):
        return (a + bit) % 2

    def query_start(i):
        x2 = 2 * flip(x // 2, i // 32) + flip(x % 2, (i // 4) % 2)
        y2 = 2 * flip(y // 2, (i // 16) % 2) + flip(y % 2, (i // 8) % 2)
        to = (y2 * 4 + x2) * 4 + (zh + i) % 4
        src, dst = main_copy(to)[1]
        send(src, dst, ss(R_Q), rs(R_QS + i // 16), zl, to * 2 + c).start()

    src, dst = main_copy(chip)[1]
    pltpu.make_async_copy(src, dst, rs(R_QS)).start()

    @pl.loop(1, 16)
    def _(i):
        query_start(i)

    slab = left.at[:, pl.ds(x * 16, 16)]
    wait_for(slab, rs(R_LEFT))
    for j in range(1, 4):
        send(slab, slab, ss(R_AG), rs(R_AG), zl, seq_of(y, (x + j) % 4, zh, c)).start()

    @pl.loop(16, 64)
    def _(i):
        query_start(i)

    w_slab = w_buf.at[c, pl.ds(y * 4, 4)]
    wait_for(w_slab, rs(R_WX))
    w_own_fwd = send(w_slab, w_slab, ss(R_WSIB), rs(R_WSIB), zl, sib)
    w_own_fwd.start()

    for j in range(1, 4):
        send(w_slab, w_slab, ss(R_W), rs(R_W), zl, seq_of((y + j) % 4, x, zh, c)).start()

    for i in range(4):
        down_all[i] = joined(down_v[i].astype(F32), down_sib[i].astype(F32))
    loads[5].wait()
    place = lax.broadcasted_iota(jnp.int32, (1, 2560), 1).astype(F32)
    angles = timestep[0].astype(F32) * jnp.exp(place * (-math.log(10000.0) / 2560))
    loads[6].wait()
    gate[...] = gate[...] + jnp.where(zl == 0, jnp.cos(angles), jnp.sin(angles))
    for i in range(4):
        up_cat[64 * i : 64 * (i + 1), :] = up_v[adapter[i]]

    wait_for(left_q, rs(R_LEFTQ))
    wait_for(left.at[:, pl.ds(0, 48)], rs(R_AG))
    ag_sib = send(left, left_sib, ss(R_AGSIB), rs(R_AGSIB), zl, sib)
    ag_sib.start()
    main_kv = main.at[pl.ds(1, 2)]
    wait_for(main_kv, rs(R_MAIN))
    kv_sib = send(main_kv, main_sib, ss(R_KVSIB), rs(R_KVSIB), zl, sib)
    kv_sib.start()
    wait_for(left_sib, rs(R_AGSIB))

    def attend(q, keys, values, tile):
        q = q.reshape(256, 128)
        scores = [
            lax.dot_general(q, k.reshape(1024, 128), (((1,), (1,)), ((), ())), preferred_element_type=F32)
            * SCORE_SCALE
            for k in keys
        ]
        top = jnp.maximum(
            jnp.max(scores[0], axis=1, keepdims=True), jnp.max(scores[1], axis=1, keepdims=True)
        )
        total = 0.0
        mixed = 0.0
        for half in range(2):
            weights = jnp.exp2(scores[half] - top)
            total = total + jnp.sum(weights, axis=1, keepdims=True)
            mixed = mixed + jnp.dot(
                weights.astype(BF16), values[half].reshape(1024, 128), preferred_element_type=F32
            )
        o_t[:, pl.ds(pl.multiple_of(tile * 256, 256), 256)] = jnp.transpose(mixed / total).astype(BF16)

    def attend_main(tile):
        attend(main[0, pl.ds(tile * 16, 16)], (main[1], main_sib[0]), (main[2], main_sib[1]), tile)

    places = (
        ((0, 0), ((0, 80, 0, 0), (80, 48, 1, 0))),
        ((0, 1), ((0, 32, 1, 48), (32, 80, 2, 0), (112, 16, 3, 0))),
        ((1, 0), ((0, 16, 0, 64), (16, 80, 1, 0), (96, 32, 2, 0))),
        ((1, 1), ((0, 48, 2, 32), (48, 80, 3, 0))),
    )
    pair_all = 2 * zl + zh % 2

    def m1_each(tile, action):
        core2 = tile // 2
        lanes = pl.ds(pl.multiple_of((tile % 2) * 256, 256), 256)
        for (odd, which), pieces in places:

            @pl.when(jnp.logical_and(x % 2 == odd, zh // 2 == which))
            def _():
                for first, count, z2, row in pieces:
                    src = o_t.at[pl.ds(first, count), pl.ds(pl.multiple_of(tile * 256, 256), 256)]
                    dst = m1.at[pair_all, pl.ds(row, count), lanes]
                    mine = jnp.logical_and(jnp.logical_and(z2 == zh, c == zl), core2 == c)
                    action(src, dst, mine, seq_of(y, x, z2, core2))

    def m1_start(src, dst, mine, to):
        @pl.when(mine)
        def _():
            pltpu.make_async_copy(src, dst, rs(R_M1)).start()

        @pl.when(jnp.logical_not(mine))
        def _():
            send(src, dst, ss(R_M1), rs(R_M1), c, to).start()

    def m1_wait_send(src, dst, mine, to):
        @pl.when(jnp.logical_not(mine))
        def _():
            send(src, dst, ss(R_M1), rs(R_M1), c, to).wait_send()

    def m1_left_copy(i):
        odd = i % 2
        core2 = i // 2
        src = o_t.at[
            pl.ds(pl.multiple_of(odd * 64, 16), 64), pl.ds(pl.multiple_of(1024 + core2 * 128, 128), 128)
        ]
        dst = m1.at[
            pair_all, pl.ds(pl.multiple_of(16 * (1 - odd), 16), 64), pl.ds(pl.multiple_of(x * 128, 128), 128)
        ]
        return src, dst, 2 * (zh // 2) + odd, 3 * (1 - odd), core2

    def left_mine(x2, z2, core2):
        here = jnp.logical_and(x2 == x, z2 == zh)
        return jnp.logical_and(here, jnp.logical_and(c == zl, core2 == c))

    def m1_left_start(i):
        src, dst, x2, z2, core2 = m1_left_copy(i)
        mine = left_mine(x2, z2, core2)

        @pl.when(mine)
        def _():
            pltpu.make_async_copy(src, dst, rs(R_M1)).start()

        @pl.when(jnp.logical_not(mine))
        def _():
            send(src, dst, ss(R_M1), rs(R_M1), c, seq_of(y, x2, z2, core2)).start()

    def m1_left_wait_send(i):
        src, dst, x2, z2, core2 = m1_left_copy(i)

        @pl.when(jnp.logical_not(left_mine(x2, z2, core2)))
        def _():
            send(src, dst, ss(R_M1), rs(R_M1), c, seq_of(y, x2, z2, core2)).wait_send()

    pl.semaphore_wait(token, 1)
    attend(left_q[...], (left[0], left_sib[0]), (left[1], left_sib[1]), 4)

    @pl.loop(0, 4)
    def _(i):
        m1_left_start(i)

    wait_for(main_sib, rs(R_KVSIB))

    @pl.loop(0, 4)
    def _(t):
        tile = 2 * flip(x // 2, t // 2) + flip(y // 2, t % 2)
        wait_for(main.at[0, pl.ds(0, 16)], rs(R_QS + t))
        attend_main(tile)

        m1_each(tile, m1_start)

    wait_for(m1, rs(R_M1))
    guide = [weight_eighths[i].astype(F32) * GUIDE_UNIT for i in range(4)]
    total = m1[0].astype(F32) * guide[0]
    for i in range(1, 4):
        total = total + m1[i].astype(F32) * guide[i]
    mx[...] = total.astype(BF16)

    def m2_copy(i):
        src = mx.at[:, pl.ds(pl.multiple_of((i // 4) * 128, 128), 128)]
        return src, m2.at[col]

    @pl.loop(1, 16)
    def _(j):
        i = (col + j) % 16
        src, dst = m2_copy(i)
        send(src, dst, ss(R_M2), rs(R_M2), zl, seq_of(i // 4, i % 4, zh, c)).start()

    src, dst = m2_copy(col)
    pltpu.make_async_copy(src, dst, rs(R_M2)).start()

    wait_for(w_buf.at[0, pl.ds(0, 12)], rs(R_W))

    def w_fwd(j):
        rows = w_buf.at[c, pl.ds((y + j) % 4 * 4, 4)]
        return send(rows, rows, ss(R_WSIB), rs(R_WSIB), zl, sib)

    for j in range(1, 4):
        w_fwd(j).start()

    ranks = jnp.concatenate(
        [
            lax.dot_general(
                down_all[adapter[i]], m1[i], (((0,), (0,)), ((), ())), preferred_element_type=F32
            )
            * guide[i]
            for i in range(4)
        ],
        axis=0,
    )
    lr[...] = jnp.transpose(ranks).astype(BF16)

    def lr_copy(i):
        src = lr.at[pl.ds(pl.multiple_of(i * 32, 32), 32)]
        return src, lr_got.at[col]

    @pl.loop(1, 16)
    def _(j):
        i = (col + j) % 16
        src, dst = lr_copy(i)
        send(src, dst, ss(R_LR), rs(R_LR), zl, seq_of(i // 4, i % 4, zh, c)).start()

    src, dst = lr_copy(col)
    pltpu.make_async_copy(src, dst, rs(R_LR)).start()

    wait_for(w_buf.at[0], rs(R_WSIB))
    wait_for(m2, rs(R_M2))
    rows = jnp.transpose(m2[...].reshape(1280, 128).astype(F32)).astype(BF16)
    def project(half):
        p_out[:, 640 * half : 640 * (half + 1)] = jnp.dot(
            rows, w_buf[half].reshape(1280, 640), preferred_element_type=F32
        ).astype(BF16)

    def p_copy(i, half):
        x2 = 2 * c + i // 4
        z2 = i % 4
        src = p_out.at[pl.ds(pl.multiple_of(i * 16, 16), 16), pl.ds(640 * half, 640)]
        dst = p_got.at[zh, :, pl.ds(pl.multiple_of(640 * x, 128), 640)]
        here = jnp.logical_and(jnp.logical_and(x2 == x, z2 == zh), zl == half)
        return src, dst, seq_of(y, x2, z2, zl), jnp.logical_and(here, c == zl)

    def p_start(half):
        @pl.loop(0, 8)
        def _(i):
            src, dst, to, mine = p_copy(i, half)

            @pl.when(mine)
            def _():
                pltpu.make_async_copy(src, dst, rs(R_P)).start()

            @pl.when(jnp.logical_not(mine))
            def _():
                send(src, dst, ss(R_P), rs(R_P), half, to).start()

    project(0)
    p_start(0)
    project(1)
    p_start(1)

    wait_for(lr_got, rs(R_LR))
    low = lr_got[0].astype(F32)
    for i in range(1, 16):
        low = low + lr_got[i].astype(F32)
    lr_sum[...] = low.astype(BF16)

    def lrf_copy(i):
        x2 = 2 * c + x // 2
        z2 = 2 * (x % 2) + i // 2
        zl2 = i % 2
        src = lr_sum.at[pl.ds(pl.multiple_of((i // 2) * 16, 16), 16)]
        dst = lr_fin.at[zh]
        here = jnp.logical_and(jnp.logical_and(x2 == x, z2 == zh), zl2 == zl)
        return src, dst, zl2, seq_of(y, x2, z2, zl), jnp.logical_and(here, c == zl)

    @pl.loop(0, 4)
    def _(i):
        src, dst, zl2, to, mine = lrf_copy(i)

        @pl.when(mine)
        def _():
            pltpu.make_async_copy(src, dst, rs(R_LRF)).start()

        @pl.when(jnp.logical_not(mine))
        def _():
            send(src, dst, ss(R_LRF), rs(R_LRF), zl2, to).start()

    wait_for(lr_fin, rs(R_LRF))
    low = lr_fin[0].astype(F32)
    for i in range(1, 4):
        low = low + lr_fin[i].astype(F32)
    adapted = jnp.dot(low.astype(BF16), up_cat[...], preferred_element_type=F32)
    wait_for(p_got, rs(R_P))
    for i in range(4):
        adapted = adapted + p_got[i].astype(F32)
    out[...] = (adapted * gate[...]).astype(BF16)

    for copy in sib_copies:
        copy.wait_send()
    wait_for(left.at[:, pl.ds(0, 15)], ss(R_LEFT))
    wait_for(left_q.at[pl.ds(0, 15)], ss(R_LEFTQ))

    @pl.when(x != y)
    def _():
        left_q_far.wait_send()

    wait_for(main.at[pl.ds(1, 2), pl.ds(0, 63)], ss(R_MAIN))
    wait_for(main.at[0, pl.ds(0, 63)], ss(R_Q))
    wait_for(w_buf.at[0, pl.ds(0, 3)], ss(R_WX))
    wait_for(w_buf.at[0, pl.ds(0, 12)], ss(R_W))
    wait_for(left.at[:, pl.ds(0, 48)], ss(R_AG))
    ag_sib.wait_send()
    kv_sib.wait_send()
    wait_for(w_buf.at[0], ss(R_WSIB))

    @pl.loop(0, 4)
    def _(tile):
        m1_each(tile, m1_wait_send)

    @pl.loop(0, 4)
    def _(i):
        m1_left_wait_send(i)

    wait_for(m2.at[pl.ds(0, 15)], ss(R_M2))
    wait_for(lr_got.at[pl.ds(0, 15)], ss(R_LR))

    for half in range(2):

        @pl.loop(0, 8)
        def _(i):
            src, dst, to, mine = p_copy(i, half)

            @pl.when(jnp.logical_not(mine))
            def _():
                send(src, dst, ss(R_P), rs(R_P), half, to).wait_send()

    @pl.loop(0, 4)
    def _(i):
        src, dst, zl2, to, mine = lrf_copy(i)

        @pl.when(jnp.logical_not(mine))
        def _():
            send(src, dst, ss(R_LRF), rs(R_LRF), zl2, to).wait_send()


def shards(q, k, v, w, down, up, adapter, weight_eighths, gate_offset, timestep):
    whole = pl.BlockSpec(memory_space=pl.ANY)
    smem = pl.BlockSpec(memory_space=pltpu.SMEM)
    vm = pltpu.VMEM
    return pl.pallas_call(
        body,
        out_shape=jax.ShapeDtypeStruct((16, 2560), BF16),
        in_specs=[smem] * 3 + [whole] * 7,
        out_specs=pl.BlockSpec(memory_space=pltpu.VMEM),
        scratch_shapes=[
            vm((3, 2, 16, 5120), BF16),
            vm((40, 5120), BF16),
            vm((4, 40, 640), BF16),
            vm((4, 80, 640), BF16),
            vm((2, 16, 80, 640), BF16),
            vm((4, 40, 64), BF16),
            vm((4, 40, 64), BF16),
            vm((4, 80, 64), BF16),
            vm((4, 64, 2560), BF16),
            vm((256, 2560), BF16),
            vm((3, 64, 16, 128), BF16),
            vm((2, 64, 16, 128), BF16),
            vm((16, 16, 128), BF16),
            vm((2, 64, 16, 128), BF16),
            vm((2, 64, 16, 128), BF16),
            vm((128, 1280), BF16),
            vm((4, 80, 512), BF16),
            vm((80, 512), BF16),
            vm((16, 80, 128), BF16),
            vm((512, 256), BF16),
            vm((16, 32, 256), BF16),
            vm((32, 256), BF16),
            vm((128, 1280), BF16),
            vm((4, 16, 2560), BF16),
            vm((4, 16, 256), BF16),
            vm((1, 2560), F32),
            pltpu.SemaphoreType.DMA((7,)),
            pltpu.SemaphoreType.DMA((17,)),
            pltpu.SemaphoreType.DMA((21,)),
            pltpu.SemaphoreType.REGULAR,
        ],
        compiler_params=pltpu.CompilerParams(
            collective_id=0, has_side_effects=True, vmem_limit_bytes=62 * 2**20
        ),
        name="guided_attention",
    )(adapter, weight_eighths, timestep, gate_offset, q, k, v, w, down, up)


def solution(mesh):
    placed = (
        P("branch", "seq", None),
        P("branch", "seq", None),
        P("branch", "seq", None),
        P("seq", None),
        P(None, "seq", None),
        P(),
        P(),
        P(),
        P("branch"),
        P(),
    )
    return jax.shard_map(
        shards, mesh=mesh, in_specs=placed, out_specs=P("seq", "branch"), check_vma=False
    )
```
